768 devices in a mesh: space: 64 (over x, y, core), feat: 12 (over z).
Axes of the slice: x: 4, y: 8, z: 12, core: 2. Of those that a mesh axis runs over, the one named last changes fastest.
Arguments:
- grid_latents: bfloat16 [196608, 512], P(('space', 'feat')), may hold values from -6 to 6
- grid_region: int32 [196608, 1], P(('space', 'feat')), may hold values from 0 to 63; in each aligned block of 256 rows (0 to 255, 256 to 511, ...) at most 8 rows name the same one
- grid_node: int32 [196608], P(('space', 'feat')), may hold values from 0 to 191
- mesh_latents: bfloat16 [12288, 512], P('space'), may hold values from -6 to 6
- edge_latents: bfloat16 [294912, 512], P(('space', 'feat')), may hold values from -6 to 6
- edge_sender: int32 [294912], P(('space', 'feat')), may hold values from 0 to 959, as said below
- edge_receiver: int32 [294912], P(('space', 'feat')), may hold values from 0 to 191
- halo_send: int32 [64, 64, 12], P('space'), may hold values from 0 to 191
- w_grid: bfloat16 [512, 512], replicated, may hold values from -0.25 to 0.25
- w_edge_in: bfloat16 [1536, 512], replicated, may hold values from -0.15625 to 0.15625
- w_edge_out: bfloat16 [512, 512], replicated, may hold values from -0.25 to 0.25
- w_node_in: bfloat16 [1536, 512], replicated, may hold values from -0.15625 to 0.15625
- w_node_out: bfloat16 [512, 512], replicated, may hold values from -0.25 to 0.25
- cot_mesh: bfloat16 [12288, 512], P('space'), may hold values from -6 to 6
- cot_edges: bfloat16 [294912, 512], P(('space', 'feat')), may hold values from -6 to 6
Outputs:
- new_mesh: bfloat16 [12288, 512], P('space')
- new_edges: bfloat16 [294912, 512], P(('space', 'feat'))
- grad_mesh: bfloat16 [12288, 512], P(('space', 'feat'))
- grad_edges: bfloat16 [294912, 512], P(('space', 'feat'))
The draws below stay inside these ranges and needn't reach their ends.
Inputs may be any that keep to these rules, and one draw needn't show every extreme that they name: `grid_region`: in the 256 grid rows of one device no region is named by more than 8 rows, a bound that some block reaches. `edge_sender`: rows 0 to 191 of the lookup table are the edge's own region's nodes; row 192 + p * 12 + k is halo row k sent by region p.
All inputs are finite; a program needn't handle non-finite values.
Results may differ from the reference program's by a relative error of at most 0.027.
Values may be sent and summed in bfloat16 or wider, within the bound.
No kernel may reach another device: no remote copies, remote signals or barrier semaphores. Data moves between devices by JAX's collectives and lax.ppermute only.
A program may use at most 64 MiB of HBM per device.

```python
import math
import jax
import jax.numpy as jnp
import numpy as np
from jax import lax

D = 512
NODE_REG = 192
E_DEV = 384
G_DEV = 256
HALO_BLK = 12
CAP = 8
NODES = 12288
EDGE_REG = 4608
EDGES = 294912
GRID = 196608
N_SPACE = 64
N_FEAT = 12


def draw_edge_sender(key, part):
    key = jax.random.fold_in(key, 11)
    keys = jax.random.split(key, 7)
    count = N_SPACE * N_FEAT * E_DEV
    reach = max(1, N_SPACE // 2 - 1)
    region = jnp.arange(count, dtype=jnp.int32) // (N_FEAT * E_DEV)
    local = jax.random.randint(keys[0], (count,), 0, NODE_REG)
    distance = 1 + jnp.minimum(jax.random.randint(keys[1], (count,), 0, reach), jax.random.randint(keys[2], (count,), 0, reach))
    opposite = jax.random.randint(keys[6], (count,), 0, 4) == 0
    distance = jnp.where(opposite, N_SPACE // 2, distance)
    direction = 2 * jax.random.randint(keys[3], (count,), 0, 2) - 1
    peer = (region + direction * distance) % N_SPACE
    remote = NODE_REG + peer * HALO_BLK + jax.random.randint(keys[4], (count,), 0, HALO_BLK)
    chosen = jnp.where(jax.random.randint(keys[5], (count,), 0, 2) == 0, local, remote)
    leading = jnp.arange(count, dtype=jnp.int32) % E_DEV == 0
    return jnp.where(leading, NODE_REG + N_SPACE * HALO_BLK - 1, chosen).astype(jnp.int32)


def plant(result, key, least, top_value):
    index_at = [jax.random.randint(jax.random.fold_in(key, axis), (), 0, length) for axis, length in enumerate(result.shape)]
    longest = result.shape.index(max(result.shape))
    next_to = index_at[:longest] + [(index_at[longest] + 1) % result.shape[longest]] + index_at[longest + 1:]
    return result.at[tuple(index_at)].set(least).at[tuple(next_to)].set(top_value)


def block_scale(stream_key, shape, pieces, smallest, top_value):
    loudness = 1.0
    for dim, blocks in pieces:
        heights = jax.random.uniform(jax.random.fold_in(jax.random.fold_in(stream_key, 6), dim), (blocks,), jnp.float32, smallest / len(pieces), top_value / len(pieces))
        loudness = loudness * jnp.repeat(jnp.exp(heights), shape[dim] // blocks).reshape((-1,) + (1,) * (len(shape) - 1 - dim))
    return loudness


def assign_block(stream_key, own, number, rows, number_of, top, most, lean):
    order = jax.random.permutation(stream_key, number_of)
    packed, usual = load_shares(number_of, rows * top, most, lean, True), load_shares(number_of, rows * top, most, lean, False)
    places = jnp.arange(number_of)

    def named(tallies, rotation):
        used = int((tallies > 0).sum())
        fixed = max(1, used // 4)
        passed = fixed + (places - fixed + rotation * (used - fixed)) % max(1, number_of - fixed)
        return jnp.zeros((number_of,), jnp.int32).at[order[jnp.where(places < fixed, places, passed)]].set(jnp.asarray(tallies, jnp.int32))

    tallies = jnp.where(number % 4 == 0, named(packed, number // 4), named(usual, number - number // 4 - 1))
    mixed = jax.random.permutation(jax.random.fold_in(own, 3), number_of)
    source_of, taker = mixed[0:number_of // 2 * 2:2], mixed[1:number_of // 2 * 2:2]
    room = jnp.minimum(tallies[source_of] - 1, most - tallies[taker]) // 2
    room = jnp.where((source_of == order[0]) | (taker == order[0]) | (tallies[taker] == 0), 0, jnp.maximum(room, 0))
    passed = jax.random.randint(jax.random.fold_in(own, 4), (number_of // 2,), 0, 1 << 20) % (room + 1)
    tallies = tallies.at[source_of].add(-passed).at[taker].add(passed)
    items = jnp.searchsorted(jnp.cumsum(tallies), jnp.arange(rows * top), side="right").astype(jnp.int32)
    table = items.reshape(top, rows).T
    table = table[jax.random.permutation(jax.random.fold_in(own, 1), rows)]
    rotation = jax.random.randint(jax.random.fold_in(own, 2), (rows, 1), 0, top)
    return jnp.take_along_axis(table, (jnp.arange(top)[None, :] + rotation) % top, axis=1)


def load_shares(number_of, total, most, slope, full):
    loads = [(1 << 20) // math.isqrt(grade ** slope) + 1 for grade in range(1, number_of + 1)]
    largest = most if full else min(most, max(-(-total // number_of), total * loads[0] // sum(loads)))
    least = 1 if total - largest >= number_of - 1 else 0
    holding, rest = [largest] + [least] * (number_of - 1), total - largest - least * (number_of - 1)
    while rest > 0:
        free = [i for i in range(1, number_of) if holding[i] < largest] or [i for i in range(1, number_of) if holding[i] < most]
        whole, remaining = sum([loads[i] for i in free]), rest
        for i in free:
            addition = min(most - holding[i], max(1, remaining * loads[i] // whole), rest)
            holding[i] = holding[i] + addition
            rest = rest - addition
    return np.array(holding)


def noise(key, shape, width, most, cuts=(), held_as=jnp.bfloat16):
    gain = block_scale(key, shape, cuts, -0.22, 0.18) if cuts else 1.0
    array = jax.random.normal(key, shape, jnp.float32) * width * gain
    return jnp.minimum(jnp.maximum(array, -most), most).astype(held_as)


def setup_inputs(seed: int = 0) -> dict:
    seeds = jax.random.split(jax.random.key(seed), 16)
    grid_latents = noise(seeds[0], (GRID, D), 1.0, 6.0, ((0, 768),))
    grid_region_keys = jax.random.split(jax.random.fold_in(seeds[1], 1), GRID // G_DEV)
    grid_region_turns = jax.random.permutation(jax.random.fold_in(seeds[1], 3), GRID // G_DEV)
    grid_region = jax.vmap(lambda own, number: assign_block(jax.random.fold_in(seeds[1], 2), own, number, G_DEV, N_SPACE, 1, CAP, 2))(grid_region_keys, grid_region_turns).reshape((GRID, 1))
    grid_node = plant(jax.random.randint(seeds[2], (GRID,), 0, NODE_REG), jax.random.fold_in(seeds[2], 1), 0, NODE_REG - 1).astype(jnp.int32)
    mesh_latents = noise(seeds[3], (NODES, D), 1.0, 6.0, ((0, 64),))
    edge_latents = noise(seeds[4], (EDGES, D), 1.0, 6.0, ((0, 768),))
    edge_sender = draw_edge_sender(jax.random.fold_in(seeds[15], 71), 0)
    edge_receiver = plant(jax.random.randint(seeds[6], (EDGES,), 0, NODE_REG), jax.random.fold_in(seeds[6], 1), 0, NODE_REG - 1).astype(jnp.int32)
    halo_send = plant(jax.random.randint(seeds[7], (N_SPACE, N_SPACE, HALO_BLK), 0, NODE_REG), jax.random.fold_in(seeds[7], 1), 0, NODE_REG - 1).astype(jnp.int32)
    w_grid = noise(seeds[8], (D, D), D ** -0.5, 0.25)
    w_edge_in = noise(seeds[9], (3 * D, D), (3 * D) ** -0.5, 0.15625)
    w_edge_out = noise(seeds[10], (D, D), D ** -0.5, 0.25)
    w_node_in = noise(seeds[11], (3 * D, D), (3 * D) ** -0.5, 0.15625)
    w_node_out = noise(seeds[12], (D, D), D ** -0.5, 0.25)
    cot_mesh = noise(seeds[13], (NODES, D), 1.0, 6.0, ((0, 64),))
    cot_edges = noise(seeds[14], (EDGES, D), 1.0, 6.0, ((0, 768),))
    return dict(grid_latents=grid_latents, grid_region=grid_region, grid_node=grid_node, mesh_latents=mesh_latents, edge_latents=edge_latents, edge_sender=edge_sender, edge_receiver=edge_receiver, halo_send=halo_send, w_grid=w_grid, w_edge_in=w_edge_in, w_edge_out=w_edge_out, w_node_in=w_node_in, w_node_out=w_node_out, cot_mesh=cot_mesh, cot_edges=cot_edges)


def layer_norm(values):
    center = values - lax.optimization_barrier(jnp.mean(values, -1, keepdims=True))
    spread = lax.optimization_barrier(jnp.mean(center * center, -1, keepdims=True))
    return center * lax.rsqrt(spread + 1e-05)

def edge_piece(edge_rows, sender_rows, receiver_rows, w_edge_in, w_edge_out):
    joined = jnp.concatenate([edge_rows, sender_rows.astype(jnp.bfloat16), receiver_rows.astype(jnp.bfloat16)], 1)
    hidden = jax.nn.silu(jnp.dot(joined, w_edge_in, preferred_element_type=jnp.float32)).astype(jnp.bfloat16)
    update = layer_norm(jnp.dot(hidden, w_edge_out, preferred_element_type=jnp.float32))
    return (edge_rows.astype(jnp.float32) + update).astype(jnp.bfloat16)

def node_piece(mesh_wide, grid_sum, edge_sum, w_node_in, w_node_out):
    joined = jnp.concatenate([mesh_wide.astype(jnp.bfloat16), grid_sum.astype(jnp.bfloat16), edge_sum.astype(jnp.bfloat16)], 1)
    hidden = jax.nn.silu(jnp.dot(joined, w_node_in, preferred_element_type=jnp.float32)).astype(jnp.bfloat16)
    update = layer_norm(jnp.dot(hidden, w_node_out, preferred_element_type=jnp.float32))
    return (mesh_wide + update).astype(jnp.bfloat16)

def reference(grid_latents, grid_region, grid_node, mesh_latents, edge_latents, edge_sender, edge_receiver, halo_send, w_grid, w_edge_in, w_edge_out, w_node_in, w_node_out, cot_mesh, cot_edges):
    message = jax.nn.silu(jnp.dot(grid_latents, w_grid, preferred_element_type=jnp.float32)).astype(jnp.bfloat16)
    grid_target = grid_region[:, 0] * NODE_REG + grid_node
    grid_sum = jax.ops.segment_sum(message.astype(jnp.float32), grid_target, num_segments=NODES)
    region_ids = jnp.arange(N_SPACE, dtype=jnp.int32)
    halo_index = (region_ids[:, None, None] * NODE_REG + halo_send).transpose(1, 0, 2).reshape(N_SPACE, N_SPACE * HALO_BLK)
    receiver_global = jnp.arange(EDGES, dtype=jnp.int32) // EDGE_REG * NODE_REG + edge_receiver

    def one_region(region_items):
        lookup_rows, region_rows, sender_index, receiver_index, edge_rows = region_items
        return edge_piece(edge_rows, lookup_rows[sender_index], region_rows[receiver_index], w_edge_in, w_edge_out)

    def forward(mesh_input, edge_input):
        mesh_wide = mesh_input.astype(jnp.float32)
        regions = mesh_wide.reshape(N_SPACE, NODE_REG, D)
        lookup_table = jnp.concatenate([regions, mesh_wide[halo_index]], 1)
        new_edges = lax.map(jax.checkpoint(one_region), (lookup_table, regions, edge_sender.reshape(N_SPACE, EDGE_REG), edge_receiver.reshape(N_SPACE, EDGE_REG), edge_input.reshape(N_SPACE, EDGE_REG, D))).reshape(EDGES, D)
        edge_sum = jax.ops.segment_sum(new_edges.astype(jnp.float32), receiver_global, num_segments=NODES)
        new_mesh = node_piece(mesh_wide, grid_sum, edge_sum, w_node_in, w_node_out)
        return (new_mesh, new_edges)
    (new_mesh, new_edges), backward = jax.vjp(forward, mesh_latents, edge_latents)
    grad_mesh, grad_edges = backward((cot_mesh, cot_edges))
    return (new_mesh, new_edges, grad_mesh, grad_edges)
```

```python
import functools

import jax
import jax.numpy as jnp
from jax import lax
from jax.experimental import pallas as pl
from jax.experimental.pallas import tpu as pltpu
from jax.sharding import PartitionSpec as P

BF = jnp.bfloat16
F32 = jnp.float32
VMEM_BYTES = 48 * 1024 * 1024


def mm(a, b):
    return jnp.dot(a, b, preferred_element_type=F32)


def mm_nt(a, b):
    return lax.dot_general(a, b, (((1,), (1,)), ((), ())), preferred_element_type=F32)


def iota(shape, dim):
    return lax.broadcasted_iota(jnp.int32, shape, dim)


def one_hot(a, b):
    return (a == b).astype(F32).astype(BF)


def column_of(row):
    n = row.shape[1]
    eye = iota((n, n), 0) == iota((n, n), 1)
    return jnp.sum(jnp.where(eye, row.astype(F32), 0.0), axis=1, keepdims=True).astype(jnp.int32)


def halo_column(halo_t, block, offset):
    count, spaces = halo_t.shape
    rows = spaces * 8
    spread = one_hot(iota((rows, spaces), 0) // 8, iota((rows, spaces), 1))
    all_k = mm_nt(spread, halo_t.astype(F32).astype(BF))
    wanted = offset + (iota((rows, count), 0) % 8) % block
    keep = wanted == iota((rows, count), 1)
    return jnp.sum(jnp.where(keep, all_k, 0.0), axis=1, keepdims=True).astype(jnp.int32)


def halo_row(halo_t, block, offset):
    count, spaces = halo_t.shape
    rows = spaces * 8
    spread = one_hot(iota((spaces, rows), 0), iota((spaces, rows), 1) // 8)
    all_k = mm(halo_t.astype(F32).astype(BF), spread)
    wanted = offset + (iota((count, rows), 1) % 8) % block
    keep = wanted == iota((count, rows), 0)
    return jnp.sum(jnp.where(keep, all_k, 0.0), axis=0, keepdims=True).astype(jnp.int32)


def silu_parts(v):
    s = 1.0 / (1.0 + jnp.exp(-v))
    return v * s, s * (1.0 + v * (1.0 - s))


def pack_kernel(grid_ref, w_ref, region_ref, node_ref, mesh_ref, halo_ref, out_ref):
    rows, width = grid_ref.shape
    half = width // 2
    spaces = halo_ref.shape[1]
    slots = spaces * 8
    v = mm(grid_ref[...], w_ref[...])
    message = silu_parts(v)[0].astype(BF)
    region = region_ref[...]
    member = one_hot(iota((spaces, rows), 0), region)
    before = (iota((rows, rows), 0) < iota((rows, rows), 1)).astype(F32).astype(BF)
    earlier = mm(member, before)
    rank = jnp.sum(earlier * member.astype(F32), axis=0, keepdims=True).astype(jnp.int32)
    slot = region * 8 + rank
    place = iota((slots, rows), 0) == slot
    labels = jnp.sum(
        jnp.where(place, (node_ref[...] + 1).astype(F32), 0.0), axis=1, keepdims=True
    )
    out_ref[:, width + half : 2 * width + half] = mm(
        place.astype(F32).astype(BF), message
    ).astype(BF)
    out_ref[:, 2 * width + half :] = jnp.broadcast_to(labels, (slots, 128)).astype(BF)
    mesh = mesh_ref[...]
    nodes = mesh.shape[0]
    halo_t = halo_ref[...]
    first = halo_column(halo_t, 8, 0)
    out_ref[:, :width] = mm(one_hot(first, iota((slots, nodes), 1)), mesh).astype(BF)
    rest = halo_column(halo_t, 4, 8)
    tail = mm(one_hot(rest, iota((slots, nodes), 1)), mesh)
    left = iota((slots, half), 0) % 8 < 4
    out_ref[:, width : width + half] = jnp.where(left, tail[:, :half], tail[:, half:]).astype(BF)


def table_ids(shape, dim, nodes, count):
    index = iota(shape, dim)
    peer = index // 8
    j = index % 8
    base = nodes + peer * count
    whole = base + j
    tail = base + 8 + j % 4
    return whole, jnp.where(j < 4, tail, -1), jnp.where(j < 4, -1, tail)


def edge_forward_kernel(
    got_ref,
    edge_ref,
    sender_ref,
    receiver_ref,
    mesh_ref,
    w_in_ref,
    w_out_ref,
    new_ref,
    sums_ref,
    slope_ref,
    xhat_ref,
    rstd_ref,
    count,
):
    edges, width = edge_ref.shape
    half = width // 2
    nodes = mesh_ref.shape[0]
    slots = got_ref.shape[0]
    feats = sums_ref.shape[0]
    share = nodes // feats
    mesh = mesh_ref[...]
    edge = edge_ref[...]
    sender = column_of(sender_ref[...])
    receiver = column_of(receiver_ref[...])
    whole, left, right = table_ids((1, slots), 1, nodes, count)
    head = mm(one_hot(sender, iota((edges, nodes), 1)), mesh) + mm(
        one_hot(sender, whole), got_ref[:, :width]
    )
    tail = got_ref[:, width : width + half]
    tail_left = mm(one_hot(sender, left), tail)
    tail_right = mm(one_hot(sender, right), tail)
    sender_rows = (head + jnp.concatenate([tail_left, tail_right], 1)).astype(BF)
    receiver_rows = mm(one_hot(receiver, iota((edges, nodes), 1)), mesh).astype(BF)
    v = (
        mm(edge, w_in_ref[:width, :])
        + mm(sender_rows, w_in_ref[width : 2 * width, :])
        + mm(receiver_rows, w_in_ref[2 * width :, :])
    )
    act, slope = silu_parts(v)
    slope_ref[...] = slope
    u = mm(act.astype(BF), w_out_ref[...])
    center = u - jnp.mean(u, -1, keepdims=True)
    rstd = lax.rsqrt(jnp.mean(center * center, -1, keepdims=True) + 1e-05)
    xhat = center * rstd
    xhat_ref[...] = xhat
    rstd_ref[...] = jnp.broadcast_to(rstd, rstd_ref.shape)
    new = (edge.astype(F32) + xhat).astype(BF)
    new_ref[...] = new
    edge_sum = mm(one_hot(iota((nodes, edges), 0), receiver_ref[...]), new).astype(BF)
    sums_ref[:, :, :width] = edge_sum.reshape(feats, share, width)
    label = got_ref[:, 2 * width + half :].astype(F32).T[0:1, :].astype(jnp.int32)
    grid_sum = mm(
        one_hot(iota((nodes, slots), 0) + 1, label), got_ref[:, width + half : 2 * width + half]
    ).astype(BF)
    sums_ref[:, :, width:] = grid_sum.reshape(feats, share, width)


def node_kernel(
    feat_ref,
    sums_ref,
    mesh_ref,
    cot_ref,
    w_in_ref,
    w_out_ref,
    new_ref,
    spread_ref,
    own_ref,
):
    feats, share, both = sums_ref.shape
    width = both // 2
    start = pl.multiple_of(feat_ref[0] * share, share)
    mesh = mesh_ref[pl.ds(start, share), :]
    cot = cot_ref[pl.ds(start, share), :].astype(F32)
    sums = jnp.sum(sums_ref[...].astype(F32), axis=0)
    edge_sum = sums[:, :width].astype(BF)
    grid_sum = sums[:, width:].astype(BF)
    v = (
        mm(mesh, w_in_ref[:width, :])
        + mm(grid_sum, w_in_ref[width : 2 * width, :])
        + mm(edge_sum, w_in_ref[2 * width :, :])
    )
    act, slope = silu_parts(v)
    u = mm(act.astype(BF), w_out_ref[...])
    center = u - jnp.mean(u, -1, keepdims=True)
    rstd = lax.rsqrt(jnp.mean(center * center, -1, keepdims=True) + 1e-05)
    xhat = center * rstd
    new_ref[...] = (mesh.astype(F32) + xhat).astype(BF)
    du = norm_back(cot, xhat, rstd)
    dh = mm_nt(du.astype(BF), w_out_ref[...]).astype(BF)
    dv = (dh.astype(F32) * slope).astype(BF)
    sum_grad = mm_nt(dv, w_in_ref[2 * width :, :]).astype(BF)
    spread_ref[...] = jnp.broadcast_to(sum_grad[None], spread_ref.shape)
    own_ref[...] = cot + mm_nt(dv, w_in_ref[:width, :]).astype(BF).astype(F32)


def norm_back(cot, xhat, rstd):
    return rstd * (
        cot
        - jnp.mean(cot, -1, keepdims=True)
        - xhat * jnp.mean(cot * xhat, -1, keepdims=True)
    )


def edge_back_kernel(
    grads_ref,
    cot_ref,
    sender_ref,
    receiver_ref,
    slope_ref,
    xhat_ref,
    rstd_ref,
    w_in_ref,
    w_out_ref,
    new_ref,
    send_ref,
    edge_cot_ref,
    dv_ref,
    sgrad_ref,
    new_again_ref,
    nodes,
    count,
):
    new_again_ref[...] = new_ref[...]
    edges, width = cot_ref.shape
    half = width // 2
    slots = send_ref.shape[0]
    receiver = column_of(receiver_ref[...])
    spread = mm(one_hot(receiver, iota((edges, nodes), 1)), grads_ref[...])
    cot = (cot_ref[...].astype(F32) + spread).astype(BF)
    edge_cot_ref[...] = cot
    du = norm_back(cot.astype(F32), xhat_ref[...], rstd_ref[:, 0:1])
    dh = mm_nt(du.astype(BF), w_out_ref[...]).astype(BF)
    dv = (dh.astype(F32) * slope_ref[...]).astype(BF)
    dv_ref[...] = dv
    sgrad = mm_nt(dv, w_in_ref[width : 2 * width, :]).astype(BF)
    sgrad_ref[...] = sgrad
    whole, left, right = table_ids((slots, 1), 0, nodes, count)
    sender = sender_ref[...]
    send_ref[:, :width] = mm(one_hot(whole, sender), sgrad).astype(BF)
    tail = mm(one_hot(jnp.maximum(left, right), sender), sgrad)
    send_ref[:, width:] = jnp.where(left >= 0, tail[:, :half], tail[:, half:]).astype(BF)


def edge_rest_kernel(
    edge_cot_ref, dv_ref, sgrad_ref, sender_ref, receiver_ref, w_in_ref, grad_ref, local_ref
):
    edges, width = dv_ref.shape
    nodes = local_ref.shape[0]
    dv = dv_ref[...]
    direct = mm_nt(dv, w_in_ref[:width, :]).astype(BF)
    grad_ref[...] = (edge_cot_ref[...].astype(F32) + direct.astype(F32)).astype(BF)
    rgrad = mm_nt(dv, w_in_ref[2 * width :, :]).astype(BF)
    ids = iota((nodes, edges), 0)
    local_ref[...] = mm(one_hot(ids, sender_ref[...]), sgrad_ref[...]) + mm(
        one_hot(ids, receiver_ref[...]), rgrad
    )


def return_kernel(got_ref, local_ref, halo_ref, new_ref, out_ref, new_out_ref):
    new_out_ref[...] = new_ref[...]
    nodes, width = local_ref.shape
    half = width // 2
    slots = got_ref.shape[0]
    feats, share, _ = out_ref.shape
    halo_t = halo_ref[...]
    ids = iota((nodes, slots), 0)
    total = local_ref[...] + mm(one_hot(ids, halo_row(halo_t, 8, 0)), got_ref[:, :width])
    rest = halo_row(halo_t, 4, 8)
    is_left = iota((1, slots), 1) % 8 < 4
    tail = got_ref[:, width:]
    tail_left = mm(one_hot(ids, jnp.where(is_left, rest, -1)), tail)
    tail_right = mm(one_hot(ids, jnp.where(is_left, -1, rest)), tail)
    total = total + jnp.concatenate([tail_left, tail_right], 1)
    out_ref[...] = total.astype(BF).reshape(feats, share, width)


def finish_kernel(got_ref, own_ref, out_ref):
    out_ref[...] = (jnp.sum(got_ref[...].astype(F32), axis=0) + own_ref[...]).astype(BF)


def call(kernel, outs, args, smem=0):
    vmem = pl.BlockSpec(memory_space=pltpu.VMEM)
    return pl.pallas_call(
        kernel,
        out_shape=[jax.ShapeDtypeStruct(shape, dtype) for shape, dtype in outs],
        in_specs=[pl.BlockSpec(memory_space=pltpu.SMEM)] * smem + [vmem] * (len(args) - smem),
        out_specs=[vmem] * len(outs),
        compiler_params=pltpu.CompilerParams(vmem_limit_bytes=VMEM_BYTES),
    )(*args)


def swap(values, axis):
    return lax.all_to_all(values, axis, split_axis=0, concat_axis=0, tiled=True)


def body(
    grid_latents,
    grid_region,
    grid_node,
    mesh_latents,
    edge_latents,
    edge_sender,
    edge_receiver,
    halo_send,
    w_grid,
    w_edge_in,
    w_edge_out,
    w_node_in,
    w_node_out,
    cot_mesh,
    cot_edges,
):
    spaces = lax.axis_size("space")
    feats = lax.axis_size("feat")
    feat = lax.axis_index("feat").astype(jnp.int32).reshape(1)
    nodes, width = mesh_latents.shape
    edges = edge_latents.shape[0]
    count = halo_send.shape[2]
    share = nodes // feats
    slots = spaces * 8
    wide = 2 * width + width // 2 + 128
    back = width + width // 2
    region_row = grid_region.reshape(1, -1)
    node_row = grid_node.reshape(1, -1)
    sender = edge_sender.reshape(1, -1)
    receiver = edge_receiver.reshape(1, -1)
    halo_t = halo_send[0].T

    (packed,) = call(
        pack_kernel,
        [((slots, wide), BF)],
        (grid_latents, w_grid, region_row, node_row, mesh_latents, halo_t),
    )
    got = swap(packed.reshape(spaces, 8, wide), "space").reshape(slots, wide)
    new_edges, sums, slope, xhat, rstd = call(
        functools.partial(edge_forward_kernel, count=count),
        [
            ((edges, width), BF),
            ((feats, share, 2 * width), BF),
            ((edges, width), F32),
            ((edges, width), F32),
            ((edges, 128), F32),
        ],
        (got, edge_latents, sender, receiver, mesh_latents, w_edge_in, w_edge_out),
    )
    sums = swap(sums, "feat")
    new_share, spread, own = call(
        node_kernel,
        [((share, width), BF), ((feats, share, width), BF), ((share, width), F32)],
        (feat, sums, mesh_latents, cot_mesh, w_node_in, w_node_out),
        smem=1,
    )
    grads = swap(spread, "feat").reshape(nodes, width)
    send, edge_cot, dv, sgrad, new_share = call(
        functools.partial(edge_back_kernel, nodes=nodes, count=count),
        [
            ((slots, back), BF),
            ((edges, width), BF),
            ((edges, width), BF),
            ((edges, width), BF),
            ((share, width), BF),
        ],
        (grads, cot_edges, sender, receiver, slope, xhat, rstd, w_edge_in, w_edge_out, new_share),
    )
    returned = swap(send.reshape(spaces, 8, back), "space").reshape(slots, back)
    grad_edges, local = call(
        edge_rest_kernel,
        [((edges, width), BF), ((nodes, width), F32)],
        (edge_cot, dv, sgrad, sender, receiver, w_edge_in),
    )
    new_mesh = lax.all_gather(new_share, "feat", axis=0, tiled=True)
    parts, new_mesh = call(
        return_kernel,
        [((feats, share, width), BF), ((nodes, width), BF)],
        (returned, local, halo_t, new_mesh),
    )
    (grad_mesh,) = call(finish_kernel, [((share, width), BF)], (swap(parts, "feat"), own))
    return new_mesh, new_edges, grad_mesh, grad_edges


def solution(mesh):
    return jax.shard_map(
        body,
        mesh=mesh,
        in_specs=(
            P(("space", "feat"), None),
            P(("space", "feat"), None),
            P(("space", "feat")),
            P("space", None),
            P(("space", "feat"), None),
            P(("space", "feat")),
            P(("space", "feat")),
            P("space", None, None),
            P(),
            P(),
            P(),
            P(),
            P(),
            P("space", None),
            P(("space", "feat"), None),
        ),
        out_specs=(
            P("space", None),
            P(("space", "feat"), None),
            P(("space", "feat"), None),
            P(("space", "feat"), None),
        ),
        check_vma=False,
    )
```

```python
import functools

import jax
import jax.numpy as jnp
from jax import lax
from jax.experimental import pallas as pl
from jax.experimental.pallas import tpu as pltpu
from jax.sharding import PartitionSpec as P

BF = jnp.bfloat16
F32 = jnp.float32
VMEM_BYTES = 20 * 1024 * 1024


def mm(a, b):
    return jnp.dot(a, b, preferred_element_type=F32)


def mm_nt(a, b):
    return lax.dot_general(a, b, (((1,), (1,)), ((), ())), preferred_element_type=F32)


def iota(shape, dim):
    return lax.broadcasted_iota(jnp.int32, shape, dim)


def one_hot(a, b):
    return (a == b).astype(F32).astype(BF)


def column_of(row):
    n = row.shape[1]
    eye = iota((n, n), 0) == iota((n, n), 1)
    return jnp.sum(jnp.where(eye, row.astype(F32), 0.0), axis=1, keepdims=True).astype(jnp.int32)


class Fetch:
    def __init__(self, array, rows=None, start=None, keep=False):
        self.array, self.start, self.keep = array, start, keep
        self.shape = array.shape if rows is None else (rows,) + array.shape[1:]

    def source(self, ref):
        if self.start is None:
            return ref
        return ref.at[pl.ds(self.start() if callable(self.start) else self.start, self.shape[0])]


class Push:
    def __init__(self, shape, dtype):
        self.shape, self.dtype = shape, dtype


class Late:
    def __init__(self, source, target, sem):
        self.ref, self.shape, self.waited = target, target.shape, False
        self.copy = pltpu.make_async_copy(source, target, sem)
        self.copy.start()

    def wait(self):
        if not self.waited:
            self.copy.wait()
            self.waited = True

    def __getitem__(self, index):
        self.wait()
        return self.ref[index]


class Out:
    def __init__(self, target, scratch, sems):
        self.target, self.ref, self.sems, self.copies = target, scratch, sems, []
        self.shape = scratch.shape

    def put(self, value, *columns):
        source, target = self.ref, self.target
        if columns:
            index = (slice(None),) * (len(self.shape) - 1) + (slice(*columns),)
            self.ref[index] = value
            source, target = source.at[index], target.at[index]
        else:
            self.ref[...] = value
        copy = pltpu.make_async_copy(source, target, next(self.sems))
        copy.start()
        self.copies.append(copy)

    def wait(self):
        for copy in self.copies:
            copy.wait()


def call(kernel, outs, args):
    fetches = [arg for arg in args if isinstance(arg, Fetch)]
    kept = [arg for arg in fetches if arg.keep]
    pushes = [out for out in outs if isinstance(out, Push)]
    semaphores = len(fetches) + 4 * len(pushes)

    def run(*refs):
        ins, refs = refs[: len(args)], refs[len(args) :]
        plain_outs, refs = refs[: len(outs)], refs[len(outs) :]
        kept_refs, refs = iter(refs[: len(kept)]), refs[len(kept) :]
        scratch = iter(refs)
        sems = iter([refs[-1].at[i] for i in range(semaphores)] if semaphores else [])
        given = []
        for arg, ref in zip(args, ins):
            if isinstance(arg, Fetch):
                target = next(kept_refs if arg.keep else scratch)
                ref = Late(arg.source(ref), target, next(sems))
            given.append(ref)
        for out, ref in zip(outs, plain_outs):
            given.append(Out(ref, next(scratch), sems) if isinstance(out, Push) else ref)
        kernel(*given)
        for ref in given:
            if isinstance(ref, (Late, Out)):
                ref.wait()

    vmem = pl.BlockSpec(memory_space=pltpu.VMEM)
    hbm = pl.BlockSpec(memory_space=pltpu.HBM)
    scratch = [pltpu.VMEM(arg.shape, arg.array.dtype) for arg in fetches if not arg.keep]
    scratch += [pltpu.VMEM(out.shape, out.dtype) for out in pushes]
    if semaphores:
        scratch.append(pltpu.SemaphoreType.DMA((semaphores,)))
    out_shape = [
        pltpu.HBM(out.shape, out.dtype) if isinstance(out, Push) else pltpu.VMEM(*out)
        for out in outs
    ]
    results = pl.pallas_call(
        run,
        out_shape=out_shape + [pltpu.VMEM(arg.shape, arg.array.dtype) for arg in kept],
        in_specs=[hbm if isinstance(arg, Fetch) else vmem for arg in args],
        out_specs=[hbm if isinstance(out, Push) else vmem for out in outs] + [vmem] * len(kept),
        scratch_shapes=scratch,
        compiler_params=pltpu.CompilerParams(vmem_limit_bytes=VMEM_BYTES),
    )(
        *[
            pltpu.with_memory_space_constraint(arg.array, pltpu.HBM)
            if isinstance(arg, Fetch)
            else arg
            for arg in args
        ]
    )
    return results


def halo_column(halo_t, block, offset):
    count, spaces = halo_t.shape
    rows = spaces * 8
    spread = one_hot(iota((rows, spaces), 0) // 8, iota((rows, spaces), 1))
    all_k = mm_nt(spread, halo_t.astype(F32).astype(BF))
    wanted = offset + (iota((rows, count), 0) % 8) % block
    keep = wanted == iota((rows, count), 1)
    return jnp.sum(jnp.where(keep, all_k, 0.0), axis=1, keepdims=True).astype(jnp.int32)


def halo_row(halo_t, block, offset):
    count, spaces = halo_t.shape
    rows = spaces * 8
    spread = one_hot(iota((spaces, rows), 0), iota((spaces, rows), 1) // 8)
    all_k = mm(halo_t.astype(F32).astype(BF), spread)
    wanted = offset + (iota((count, rows), 1) % 8) % block
    keep = wanted == iota((count, rows), 0)
    return jnp.sum(jnp.where(keep, all_k, 0.0), axis=0, keepdims=True).astype(jnp.int32)


def silu_parts(v):
    s = 1.0 / (1.0 + jnp.exp(-v))
    return v * s, s * (1.0 + v * (1.0 - s))


def pack_kernel(region_ref, node_ref, halo_ref, mesh_ref, w_ref, grid_ref, out_ref):
    rows, width = grid_ref.shape
    half = width // 2
    spaces = halo_ref.shape[2]
    slots = spaces * 8
    region = region_ref[...]
    member = one_hot(iota((spaces, rows), 0), region)
    before = (iota((rows, rows), 0) < iota((rows, rows), 1)).astype(F32).astype(BF)
    earlier = mm(member, before)
    rank = jnp.sum(earlier * member.astype(F32), axis=0, keepdims=True).astype(jnp.int32)
    place = iota((slots, rows), 0) == region * 8 + rank
    label = (node_ref[...] + 1).astype(F32)
    labels = jnp.sum(jnp.where(place, label, 0.0), axis=1, keepdims=True)
    wide = out_ref.shape[1]
    out_ref.put(jnp.broadcast_to(labels, (slots, 128)).astype(BF), 2 * width + half, wide)
    halo_t = halo_ref[...].reshape(halo_ref.shape[0], spaces)
    first = halo_column(halo_t, 8, 0)
    rest = halo_column(halo_t, 4, 8)
    mesh = mesh_ref[...]
    ids = iota((slots, mesh.shape[0]), 1)
    out_ref.put(mm(one_hot(first, ids), mesh).astype(BF), 0, width)
    tail = mm(one_hot(rest, ids), mesh)
    left = iota((slots, half), 0) % 8 < 4
    tail = jnp.where(left, tail[:, :half], tail[:, half:]).astype(BF)
    out_ref.put(tail, width, width + half)
    message = silu_parts(mm(grid_ref[...], w_ref[...]))[0].astype(BF)
    placed = mm(place.astype(F32).astype(BF), message).astype(BF)
    out_ref.put(placed, width + half, 2 * width + half)


def table_ids(shape, dim, nodes, count):
    index = iota(shape, dim)
    j = index % 8
    base = nodes + index // 8 * count
    tail = base + 8 + j % 4
    return base + j, jnp.where(j < 4, tail, -1), jnp.where(j < 4, -1, tail)


def ready_kernel(
    sender_ref,
    receiver_ref,
    mesh_ref,
    halo_ref,
    edge_ref,
    w_in_ref,
    base_ref,
    local_ref,
    pick_whole_ref,
    pick_left_ref,
    pick_right_ref,
    pick_receiver_ref,
    sum_receiver_ref,
    sum_sender_ref,
    send_whole_ref,
    send_tail_ref,
    back_whole_ref,
    back_left_ref,
    back_right_ref,
    count,
):
    edges, width = edge_ref.shape
    nodes = mesh_ref.shape[0]
    slots = pick_whole_ref.shape[1]
    sender_row, receiver_row = sender_ref[...], receiver_ref[...]
    sender, receiver = column_of(sender_row), column_of(receiver_row)
    ids = iota((edges, nodes), 1)
    pick_receiver = one_hot(receiver, ids)
    pick_receiver_ref.put(pick_receiver)
    mesh = mesh_ref[...]
    receiver_rows = mm(pick_receiver, mesh).astype(BF)
    local_ref.put(mm(one_hot(sender, ids), mesh).astype(BF))
    base = mm(edge_ref[...], w_in_ref[:width, :])
    base_ref.put(base + mm(receiver_rows, w_in_ref[2 * width :, :]))
    whole, left, right = table_ids((1, slots), 1, nodes, count)
    pick_whole_ref.put(one_hot(sender, whole))
    pick_left_ref.put(one_hot(sender, left))
    pick_right_ref.put(one_hot(sender, right))
    ids = iota((nodes, edges), 0)
    sum_receiver_ref.put(one_hot(ids, receiver_row))
    sum_sender_ref.put(one_hot(ids, sender_row))
    whole, left, right = table_ids((slots, 1), 0, nodes, count)
    send_whole_ref.put(one_hot(whole, sender_row))
    send_tail_ref.put(one_hot(jnp.maximum(left, right), sender_row))
    halo_t = halo_ref[...].reshape(count, slots // 8)
    ids = iota((nodes, slots), 0)
    back_whole_ref.put(one_hot(ids, halo_row(halo_t, 8, 0)))
    rest = halo_row(halo_t, 4, 8)
    is_left = iota((1, slots), 1) % 8 < 4
    back_left_ref.put(one_hot(ids, jnp.where(is_left, rest, -1)))
    back_right_ref.put(one_hot(ids, jnp.where(is_left, -1, rest)))


def edge_forward_kernel(
    got_ref,
    pick_whole_ref,
    pick_left_ref,
    pick_right_ref,
    local_ref,
    w_mid_ref,
    base_ref,
    w_out_ref,
    edge_ref,
    sum_receiver_ref,
    node_in_ref,
    node_out_ref,
    mesh_ref,
    cot_ref,
    pick_receiver_ref,
    sums_ref,
    new_ref,
    slope_ref,
    xhat_ref,
    rstd_ref,
):
    edges, width = edge_ref.shape
    half = width // 2
    slots = got_ref.shape[0]
    feats, share, _ = sums_ref.shape
    nodes = feats * share
    label = got_ref[:, 2 * width + half :].astype(F32).T[0:1, :].astype(jnp.int32)
    grid_sum = mm(
        one_hot(iota((nodes, slots), 0) + 1, label), got_ref[:, width + half : 2 * width + half]
    ).astype(BF)
    sums_ref.put(grid_sum.reshape(feats, share, width), width, 2 * width)
    head = mm(pick_whole_ref[...], got_ref[:, :width])
    tail = got_ref[:, width : width + half]
    tails = [mm(pick_left_ref[...], tail), mm(pick_right_ref[...], tail)]
    head = head + jnp.concatenate(tails, 1) + local_ref[...].astype(F32)
    v = mm(head.astype(BF), w_mid_ref[...]) + base_ref[...]
    act, slope = silu_parts(v)
    slope_ref[...] = slope
    u = mm(act.astype(BF), w_out_ref[...])
    center = u - jnp.mean(u, -1, keepdims=True)
    rstd = lax.rsqrt(jnp.mean(center * center, -1, keepdims=True) + 1e-05)
    xhat = center * rstd
    xhat_ref[...] = xhat
    rstd_ref[...] = jnp.broadcast_to(rstd, rstd_ref.shape)
    new = (edge_ref[...].astype(F32) + xhat).astype(BF)
    new_ref.put(new)
    edge_sum = mm(sum_receiver_ref[...], new).astype(BF)
    sums_ref.put(edge_sum.reshape(feats, share, width), 0, width)


def node_kernel(
    sums_ref,
    mesh_ref,
    w_in_ref,
    w_out_ref,
    cot_ref,
    cot_edges_ref,
    send_whole_ref,
    send_tail_ref,
    w_last_ref,
    sum_sender_ref,
    spread_ref,
    new_ref,
    own_ref,
):
    width = mesh_ref.shape[1]
    mesh = mesh_ref[...]
    cot = cot_ref[...].astype(F32)
    sums = jnp.sum(sums_ref[...].astype(F32), axis=0)
    edge_sum = sums[:, :width].astype(BF)
    grid_sum = sums[:, width:].astype(BF)
    v = (
        mm(mesh, w_in_ref[:width, :])
        + mm(grid_sum, w_in_ref[width : 2 * width, :])
        + mm(edge_sum, w_in_ref[2 * width :, :])
    )
    act, slope = silu_parts(v)
    u = mm(act.astype(BF), w_out_ref[...])
    center = u - jnp.mean(u, -1, keepdims=True)
    rstd = lax.rsqrt(jnp.mean(center * center, -1, keepdims=True) + 1e-05)
    xhat = center * rstd
    new_ref[...] = (mesh.astype(F32) + xhat).astype(BF)
    du = norm_back(cot, xhat, rstd)
    dh = mm_nt(du.astype(BF), w_out_ref[...]).astype(BF)
    dv = (dh.astype(F32) * slope).astype(BF)
    sum_grad = mm_nt(dv, w_in_ref[2 * width :, :]).astype(BF)
    spread_ref[...] = jnp.broadcast_to(sum_grad[None], spread_ref.shape)
    own_ref.put(cot + mm_nt(dv, w_in_ref[:width, :]).astype(BF).astype(F32))


def norm_back(cot, xhat, rstd):
    return rstd * (
        cot
        - jnp.mean(cot, -1, keepdims=True)
        - xhat * jnp.mean(cot * xhat, -1, keepdims=True)
    )


def edge_back_kernel(
    grads_ref,
    cot_ref,
    w_out_ref,
    w_mid_ref,
    pick_receiver_ref,
    xhat_ref,
    rstd_ref,
    slope_ref,
    send_whole_ref,
    send_tail_ref,
    w_last_ref,
    sum_sender_ref,
    sum_receiver_ref,
    new_ref,
    send_ref,
    edge_cot_ref,
    dv_ref,
    local_ref,
    new_again_ref,
):
    edges, width = cot_ref.shape
    half = width // 2
    slots = send_ref.shape[0]
    spread = mm(pick_receiver_ref[...], grads_ref[...])
    cot = (cot_ref[...].astype(F32) + spread).astype(BF)
    edge_cot_ref.put(cot)
    new_again_ref.put(new_ref[...])
    du = norm_back(cot.astype(F32), xhat_ref[...], rstd_ref[:, 0:1])
    dh = mm_nt(du.astype(BF), w_out_ref[...]).astype(BF)
    dv = (dh.astype(F32) * slope_ref[...]).astype(BF)
    dv_ref.put(dv)
    sgrad = mm_nt(dv, w_mid_ref[...]).astype(BF)
    send_ref.put(mm(send_whole_ref[...], sgrad).astype(BF), 0, width)
    tail = mm(send_tail_ref[...], sgrad)
    left = iota((slots, half), 0) % 8 < 4
    tail = jnp.where(left, tail[:, :half], tail[:, half:]).astype(BF)
    send_ref.put(tail, width, width + half)
    rgrad = mm_nt(dv, w_last_ref[...]).astype(BF)
    local_ref.put(mm(sum_sender_ref[...], sgrad) + mm(sum_receiver_ref[...], rgrad))


def edge_grad_kernel(parts_ref, dv_ref, w_first_ref, edge_cot_ref, grad_ref):
    direct = mm_nt(dv_ref[...], w_first_ref[...]).astype(BF)
    grad_ref.put((edge_cot_ref[...].astype(F32) + direct.astype(F32)).astype(BF))


def return_kernel(
    got_ref, whole_ref, left_ref, right_ref, local_ref, new_ref, out_ref, new_out_ref
):
    new_out_ref.put(new_ref[...])
    width = local_ref.shape[1]
    total = mm(whole_ref[...], got_ref[:, :width])
    tail = got_ref[:, width:]
    total = total + jnp.concatenate([mm(left_ref[...], tail), mm(right_ref[...], tail)], 1)
    total = total + local_ref[...]
    out_ref.put(total.astype(BF).reshape(out_ref.shape))


def finish_kernel(got_ref, own_ref, out_ref):
    out_ref.put((jnp.sum(got_ref[...].astype(F32), axis=0) + own_ref[...]).astype(BF))


def swap(values, axis):
    return lax.all_to_all(values, axis, split_axis=0, concat_axis=0, tiled=True)


def body(
    grid_latents,
    grid_region,
    grid_node,
    mesh_latents,
    edge_latents,
    edge_sender,
    edge_receiver,
    halo_send,
    w_grid,
    w_edge_in,
    w_edge_out,
    w_node_in,
    w_node_out,
    cot_mesh,
    cot_edges,
):
    spaces = lax.axis_size("space")
    feats = lax.axis_size("feat")
    nodes, width = mesh_latents.shape
    edges = edge_latents.shape[0]
    count = halo_send.shape[2]
    share = nodes // feats
    slots = spaces * 8
    back = width + width // 2
    region_row = grid_region.reshape(1, -1)
    node_row = grid_node.reshape(1, -1)
    sender = edge_sender.reshape(1, -1)
    receiver = edge_receiver.reshape(1, -1)
    halo_t = halo_send.transpose(2, 0, 1)
    wide = 2 * width + width // 2 + 128

    def own_start():
        return pl.multiple_of(lax.axis_index("feat") * share, share)

    (packed,) = call(
        pack_kernel,
        [Push((slots, wide), BF)],
        [
            Fetch(array)
            for array in (region_row, node_row, halo_t, mesh_latents, w_grid, grid_latents)
        ],
    )
    got = swap(packed.reshape(spaces, 8, wide), "space").reshape(slots, wide)
    (
        base,
        sender_local,
        pick_whole,
        pick_left,
        pick_right,
        pick_receiver,
        sum_receiver,
        sum_sender,
        send_whole,
        send_tail,
        back_whole,
        back_left,
        back_right,
    ) = call(
        functools.partial(ready_kernel, count=count),
        [Push((edges, width), F32), Push((edges, width), BF)]
        + [Push((edges, slots), BF)] * 3
        + [Push((edges, nodes), BF)]
        + [Push((nodes, edges), BF)] * 2
        + [Push((slots, edges), BF)] * 2
        + [Push((nodes, slots), BF)] * 3,
        [
            Fetch(array)
            for array in (sender, receiver, mesh_latents, halo_t, edge_latents, w_edge_in)
        ],
    )
    (
        sums,
        new_edges,
        slope,
        xhat,
        rstd,
        w_mid,
        w_out,
        sum_receiver,
        node_in,
        node_out,
        mesh_own,
        cot_own,
        pick_receiver,
    ) = call(
        edge_forward_kernel,
        [
            Push((feats, share, 2 * width), BF),
            Push((edges, width), BF),
            ((edges, width), F32),
            ((edges, width), F32),
            ((edges, 128), F32),
        ],
        [
            got,
            Fetch(pick_whole),
            Fetch(pick_left),
            Fetch(pick_right),
            Fetch(sender_local),
            Fetch(w_edge_in, rows=width, start=width, keep=True),
            Fetch(base),
            Fetch(w_edge_out, keep=True),
            Fetch(edge_latents),
            Fetch(sum_receiver, keep=True),
            Fetch(w_node_in, keep=True),
            Fetch(w_node_out, keep=True),
            Fetch(mesh_latents, rows=share, start=own_start, keep=True),
            Fetch(cot_mesh, rows=share, start=own_start, keep=True),
            Fetch(pick_receiver, keep=True),
        ],
    )
    sums = swap(sums, "feat")
    spread, new_share, own, edge_cot, send_whole, send_tail, w_last, sum_sender = call(
        node_kernel,
        [((feats, share, width), BF), ((share, width), BF), Push((share, width), F32)],
        [
            sums,
            mesh_own,
            node_in,
            node_out,
            cot_own,
            Fetch(cot_edges, keep=True),
            Fetch(send_whole, keep=True),
            Fetch(send_tail, keep=True),
            Fetch(w_edge_in, rows=width, start=2 * width, keep=True),
            Fetch(sum_sender, keep=True),
        ],
    )
    grads = swap(spread, "feat").reshape(nodes, width)
    send, edge_cot, dv, local, new_share = call(
        edge_back_kernel,
        [
            Push((slots, back), BF),
            Push((edges, width), BF),
            Push((edges, width), BF),
            Push((nodes, width), F32),
            Push((share, width), BF),
        ],
        [
            grads,
            edge_cot,
            w_out,
            w_mid,
            pick_receiver,
            xhat,
            rstd,
            slope,
            send_whole,
            send_tail,
            w_last,
            sum_sender,
            sum_receiver,
            new_share,
        ],
    )
    returned = swap(send.reshape(spaces, 8, back), "space").reshape(slots, back)
    new_mesh = lax.all_gather(new_share, "feat", axis=0, tiled=True)
    parts, new_mesh = call(
        return_kernel,
        [Push((feats, share, width), BF), Push((nodes, width), BF)],
        [
            returned,
            Fetch(back_whole),
            Fetch(back_left),
            Fetch(back_right),
            Fetch(local),
            new_mesh,
        ],
    )
    last = swap(parts, "feat")
    (grad_edges,) = call(
        edge_grad_kernel,
        [Push((edges, width), BF)],
        [
            Fetch(parts, rows=1, start=0),
            Fetch(dv),
            Fetch(w_edge_in, rows=width, start=0),
            Fetch(edge_cot),
        ],
    )
    (grad_mesh,) = call(finish_kernel, [Push((share, width), BF)], [last, Fetch(own)])
    return new_mesh, new_edges, grad_mesh, grad_edges


def solution(mesh):
    return jax.shard_map(
        body,
        mesh=mesh,
        in_specs=(
            P(("space", "feat"), None),
            P(("space", "feat"), None),
            P(("space", "feat")),
            P("space", None),
            P(("space", "feat"), None),
            P(("space", "feat")),
            P(("space", "feat")),
            P("space", None, None),
            P(),
            P(),
            P(),
            P(),
            P(),
            P("space", None),
            P(("space", "feat"), None),
        ),
        out_specs=(
            P("space", None),
            P(("space", "feat"), None),
            P(("space", "feat"), None),
            P(("space", "feat"), None),
        ),
        check_vma=False,
    )
```

```python
import functools

import jax
import jax.numpy as jnp
from jax import lax
from jax.experimental import pallas as pl
from jax.experimental.pallas import tpu as pltpu
from jax.sharding import PartitionSpec as P

BF = jnp.bfloat16
F32 = jnp.float32
VMEM_BYTES = 20 * 1024 * 1024


def mm(a, b):
    return jnp.dot(a, b, preferred_element_type=F32)


def mm_nt(a, b):
    return lax.dot_general(a, b, (((1,), (1,)), ((), ())), preferred_element_type=F32)


def iota(shape, dim):
    return lax.broadcasted_iota(jnp.int32, shape, dim)


def one_hot(a, b):
    return (a == b).astype(F32).astype(BF)


def column_of(row):
    n = row.shape[1]
    eye = iota((n, n), 0) == iota((n, n), 1)
    return jnp.sum(jnp.where(eye, row.astype(F32), 0.0), axis=1, keepdims=True).astype(jnp.int32)


class Fetch:
    def __init__(self, array, rows=None, start=None, keep=False, defer=False):
        self.array, self.start, self.keep, self.defer = array, start, keep, defer
        self.shape = array.shape if rows is None else (rows,) + array.shape[1:]

    def source(self, ref):
        if self.start is None:
            return ref
        return ref.at[pl.ds(self.start() if callable(self.start) else self.start, self.shape[0])]


class Push:
    def __init__(self, shape, dtype):
        self.shape, self.dtype = shape, dtype


class Late:
    def __init__(self, source, target, sem, defer):
        self.ref, self.shape = target, target.shape
        self.started = self.waited = False
        self.copy = pltpu.make_async_copy(source, target, sem)
        if not defer:
            self.start()

    def start(self):
        if not self.started:
            self.copy.start()
            self.started = True

    def wait(self):
        self.start()
        if not self.waited:
            self.copy.wait()
            self.waited = True

    def __getitem__(self, index):
        self.wait()
        return self.ref[index]


class Out:
    def __init__(self, target, scratch, sems):
        self.target, self.ref, self.sems, self.copies = target, scratch, sems, []
        self.shape = scratch.shape

    def put(self, value, *columns):
        source, target = self.ref, self.target
        if columns:
            index = (slice(None),) * (len(self.shape) - 1) + (slice(*columns),)
            self.ref[index] = value
            source, target = source.at[index], target.at[index]
        else:
            self.ref[...] = value
        copy = pltpu.make_async_copy(source, target, next(self.sems))
        copy.start()
        self.copies.append(copy)

    def __setitem__(self, index, value):
        self.ref[index] = value

    def finish(self):
        if not self.copies:
            self.copies.append(pltpu.make_async_copy(self.ref, self.target, next(self.sems)))
            self.copies[0].start()

    def wait(self):
        for copy in self.copies:
            copy.wait()


def call(kernel, outs, args):
    fetches = [arg for arg in args if isinstance(arg, Fetch)]
    kept = [arg for arg in fetches if arg.keep]
    pushes = [out for out in outs if isinstance(out, Push)]
    semaphores = len(fetches) + 4 * len(pushes)

    def run(*refs):
        ins, refs = refs[: len(args)], refs[len(args) :]
        plain_outs, refs = refs[: len(outs)], refs[len(outs) :]
        kept_refs, refs = iter(refs[: len(kept)]), refs[len(kept) :]
        scratch = iter(refs)
        sems = iter([refs[-1].at[i] for i in range(semaphores)] if semaphores else [])
        given = []
        for arg, ref in zip(args, ins):
            if isinstance(arg, Fetch):
                target = next(kept_refs if arg.keep else scratch)
                ref = Late(arg.source(ref), target, next(sems), arg.defer)
            given.append(ref)
        for out, ref in zip(outs, plain_outs):
            given.append(Out(ref, next(scratch), sems) if isinstance(out, Push) else ref)
        kernel(*given)
        for ref in given:
            if isinstance(ref, Out):
                ref.finish()
        for ref in given:
            if isinstance(ref, (Late, Out)):
                ref.wait()

    vmem = pl.BlockSpec(memory_space=pltpu.VMEM)
    hbm = pl.BlockSpec(memory_space=pltpu.HBM)
    scratch = [pltpu.VMEM(arg.shape, arg.array.dtype) for arg in fetches if not arg.keep]
    scratch += [pltpu.VMEM(out.shape, out.dtype) for out in pushes]
    if semaphores:
        scratch.append(pltpu.SemaphoreType.DMA((semaphores,)))
    out_shape = [
        pltpu.HBM(out.shape, out.dtype) if isinstance(out, Push) else pltpu.VMEM(*out)
        for out in outs
    ]
    results = pl.pallas_call(
        run,
        out_shape=out_shape + [pltpu.VMEM(arg.shape, arg.array.dtype) for arg in kept],
        in_specs=[hbm if isinstance(arg, Fetch) else vmem for arg in args],
        out_specs=[hbm if isinstance(out, Push) else vmem for out in outs] + [vmem] * len(kept),
        scratch_shapes=scratch,
        compiler_params=pltpu.CompilerParams(vmem_limit_bytes=VMEM_BYTES),
    )(
        *[
            pltpu.with_memory_space_constraint(arg.array, pltpu.HBM)
            if isinstance(arg, Fetch)
            else arg
            for arg in args
        ]
    )
    return results


def halo_column(halo_t, block, offset):
    count, spaces = halo_t.shape
    rows = spaces * 8
    spread = one_hot(iota((rows, spaces), 0) // 8, iota((rows, spaces), 1))
    all_k = mm_nt(spread, halo_t.astype(F32).astype(BF))
    wanted = offset + (iota((rows, count), 0) % 8) % block
    keep = wanted == iota((rows, count), 1)
    return jnp.sum(jnp.where(keep, all_k, 0.0), axis=1, keepdims=True).astype(jnp.int32)


def halo_row(halo_t, block, offset):
    count, spaces = halo_t.shape
    rows = spaces * 8
    spread = one_hot(iota((spaces, rows), 0), iota((spaces, rows), 1) // 8)
    all_k = mm(halo_t.astype(F32).astype(BF), spread)
    wanted = offset + (iota((count, rows), 1) % 8) % block
    keep = wanted == iota((count, rows), 0)
    return jnp.sum(jnp.where(keep, all_k, 0.0), axis=0, keepdims=True).astype(jnp.int32)


def silu_parts(v):
    s = 1.0 / (1.0 + jnp.exp(-v))
    return v * s, s * (1.0 + v * (1.0 - s))


def pack_kernel(region_ref, node_ref, halo_ref, mesh_ref, w_ref, grid_ref, out_ref):
    rows, width = grid_ref.shape
    half = width // 2
    spaces = halo_ref.shape[2]
    slots = spaces * 8
    region = region_ref[...]
    member = one_hot(iota((spaces, rows), 0), region)
    before = (iota((rows, rows), 0) < iota((rows, rows), 1)).astype(F32).astype(BF)
    earlier = mm(member, before)
    rank = jnp.sum(earlier * member.astype(F32), axis=0, keepdims=True).astype(jnp.int32)
    place = iota((slots, rows), 0) == region * 8 + rank
    label = (node_ref[...] + 1).astype(F32)
    labels = jnp.sum(jnp.where(place, label, 0.0), axis=1, keepdims=True)
    wide = out_ref.shape[1]
    out_ref.put(jnp.broadcast_to(labels, (slots, 128)).astype(BF), 2 * width + half, wide)
    halo_t = halo_ref[...].reshape(halo_ref.shape[0], spaces)
    first = halo_column(halo_t, 8, 0)
    rest = halo_column(halo_t, 4, 8)
    mesh = mesh_ref[...]
    ids = iota((slots, mesh.shape[0]), 1)
    out_ref.put(mm(one_hot(first, ids), mesh).astype(BF), 0, width)
    tail = mm(one_hot(rest, ids), mesh)
    left = iota((slots, half), 0) % 8 < 4
    tail = jnp.where(left, tail[:, :half], tail[:, half:]).astype(BF)
    out_ref.put(tail, width, width + half)
    message = silu_parts(mm(grid_ref[...], w_ref[...]))[0].astype(BF)
    placed = mm(place.astype(F32).astype(BF), message).astype(BF)
    out_ref.put(placed, width + half, 2 * width + half)


def table_ids(shape, dim, nodes, count):
    index = iota(shape, dim)
    j = index % 8
    base = nodes + index // 8 * count
    tail = base + 8 + j % 4
    return base + j, jnp.where(j < 4, tail, -1), jnp.where(j < 4, -1, tail)


def ready_kernel(sender_ref, receiver_ref, mesh_ref, edge_ref, w_in_ref, base_ref, local_ref):
    edges, width = edge_ref.shape
    nodes = mesh_ref.shape[0]
    ids = iota((edges, nodes), 1)
    mesh = mesh_ref[...]
    receiver_rows = mm(one_hot(column_of(receiver_ref[...]), ids), mesh).astype(BF)
    local_ref.put(mm(one_hot(column_of(sender_ref[...]), ids), mesh).astype(BF))
    base = mm(edge_ref[...], w_in_ref[:width, :])
    base_ref.put(base + mm(receiver_rows, w_in_ref[2 * width :, :]))


def edge_forward_kernel(
    got_ref,
    sender_ref,
    receiver_ref,
    local_ref,
    w_mid_ref,
    base_ref,
    w_out_ref,
    edge_ref,
    mesh_ref,
    cot_ref,
    node_in_ref,
    node_out_ref,
    cot_edges_ref,
    sums_ref,
    new_ref,
    slope_ref,
    xhat_ref,
    rstd_ref,
    count,
):
    edges, width = edge_ref.shape
    half = width // 2
    slots = got_ref.shape[0]
    feats, share, _ = sums_ref.shape
    nodes = feats * share
    label = got_ref[:, 2 * width + half :].astype(F32).T[0:1, :].astype(jnp.int32)
    grid_sum = mm(
        one_hot(iota((nodes, slots), 0) + 1, label), got_ref[:, width + half : 2 * width + half]
    ).astype(BF)
    sums_ref[:, :, width:] = grid_sum.reshape(feats, share, width)
    sender = column_of(sender_ref[...])
    whole, left, right = table_ids((1, slots), 1, nodes, count)
    head = mm(one_hot(sender, whole), got_ref[:, :width])
    tail = got_ref[:, width : width + half]
    tails = [mm(one_hot(sender, left), tail), mm(one_hot(sender, right), tail)]
    for later in (mesh_ref, cot_ref, node_in_ref, node_out_ref, cot_edges_ref):
        later.start()
    head = head + jnp.concatenate(tails, 1) + local_ref[...].astype(F32)
    v = mm(head.astype(BF), w_mid_ref[...]) + base_ref[...]
    act, slope = silu_parts(v)
    slope_ref[...] = slope
    u = mm(act.astype(BF), w_out_ref[...])
    center = u - jnp.mean(u, -1, keepdims=True)
    rstd = lax.rsqrt(jnp.mean(center * center, -1, keepdims=True) + 1e-05)
    xhat = center * rstd
    xhat_ref[...] = xhat
    rstd_ref[...] = jnp.broadcast_to(rstd, rstd_ref.shape)
    new = (edge_ref[...].astype(F32) + xhat).astype(BF)
    new_ref.put(new)
    to_receiver = one_hot(iota((nodes, edges), 0), receiver_ref[...])
    edge_sum = mm(to_receiver, new).astype(BF)
    sums_ref[:, :, :width] = edge_sum.reshape(feats, share, width)


def node_kernel(
    sums_ref,
    mesh_ref,
    w_in_ref,
    w_out_ref,
    cot_ref,
    w_first_ref,
    w_last_ref,
    spread_ref,
    new_ref,
    own_ref,
):
    width = mesh_ref.shape[1]
    mesh = mesh_ref[...]
    cot = cot_ref[...].astype(F32)
    sums = jnp.sum(sums_ref[...].astype(F32), axis=0)
    edge_sum = sums[:, :width].astype(BF)
    grid_sum = sums[:, width:].astype(BF)
    v = (
        mm(mesh, w_in_ref[:width, :])
        + mm(grid_sum, w_in_ref[width : 2 * width, :])
        + mm(edge_sum, w_in_ref[2 * width :, :])
    )
    act, slope = silu_parts(v)
    u = mm(act.astype(BF), w_out_ref[...])
    center = u - jnp.mean(u, -1, keepdims=True)
    rstd = lax.rsqrt(jnp.mean(center * center, -1, keepdims=True) + 1e-05)
    xhat = center * rstd
    new_ref[...] = (mesh.astype(F32) + xhat).astype(BF)
    du = norm_back(cot, xhat, rstd)
    dh = mm_nt(du.astype(BF), w_out_ref[...]).astype(BF)
    dv = (dh.astype(F32) * slope).astype(BF)
    sum_grad = mm_nt(dv, w_in_ref[2 * width :, :]).astype(BF)
    spread_ref[...] = jnp.broadcast_to(sum_grad[None], spread_ref.shape)
    own_ref.put(cot + mm_nt(dv, w_in_ref[:width, :]).astype(BF).astype(F32))


def norm_back(cot, xhat, rstd):
    return rstd * (
        cot
        - jnp.mean(cot, -1, keepdims=True)
        - xhat * jnp.mean(cot * xhat, -1, keepdims=True)
    )


def edge_back_kernel(
    grads_ref,
    cot_ref,
    w_out_ref,
    w_mid_ref,
    sender_ref,
    receiver_ref,
    xhat_ref,
    rstd_ref,
    slope_ref,
    w_first_ref,
    w_last_ref,
    new_ref,
    send_ref,
    grad_ref,
    local_ref,
    new_again_ref,
    count,
):
    new_again_ref.put(new_ref[...])
    edges, width = cot_ref.shape
    half = width // 2
    nodes = grads_ref.shape[0]
    slots = send_ref.shape[0]
    sender, receiver = sender_ref[...], receiver_ref[...]
    spread = mm(one_hot(column_of(receiver), iota((edges, nodes), 1)), grads_ref[...])
    cot = (cot_ref[...].astype(F32) + spread).astype(BF)
    du = norm_back(cot.astype(F32), xhat_ref[...], rstd_ref[:, 0:1])
    dh = mm_nt(du.astype(BF), w_out_ref[...]).astype(BF)
    dv = (dh.astype(F32) * slope_ref[...]).astype(BF)
    sgrad = mm_nt(dv, w_mid_ref[...]).astype(BF)
    whole, left, right = table_ids((slots, 1), 0, nodes, count)
    send_ref.put(mm(one_hot(whole, sender), sgrad).astype(BF), 0, width)
    tail = mm(one_hot(jnp.maximum(left, right), sender), sgrad)
    tail = jnp.where(left >= 0, tail[:, :half], tail[:, half:]).astype(BF)
    send_ref.put(tail, width, width + half)
    rgrad = mm_nt(dv, w_last_ref[...]).astype(BF)
    ids = iota((nodes, edges), 0)
    local_ref.put(mm(one_hot(ids, sender), sgrad) + mm(one_hot(ids, receiver), rgrad))
    direct = mm_nt(dv, w_first_ref[...]).astype(BF)
    grad_ref.put((cot.astype(F32) + direct.astype(F32)).astype(BF))


def return_kernel(got_ref, halo_ref, local_ref, own_ref, new_ref, out_ref, new_out_ref):
    new_out_ref.put(new_ref[...])
    nodes, width = local_ref.shape
    slots = got_ref.shape[0]
    halo_t = halo_ref[...].reshape(halo_ref.shape[0], slots // 8)
    ids = iota((nodes, slots), 0)
    total = mm(one_hot(ids, halo_row(halo_t, 8, 0)), got_ref[:, :width])
    rest = halo_row(halo_t, 4, 8)
    is_left = iota((1, slots), 1) % 8 < 4
    tail = got_ref[:, width:]
    left = mm(one_hot(ids, jnp.where(is_left, rest, -1)), tail)
    right = mm(one_hot(ids, jnp.where(is_left, -1, rest)), tail)
    total = total + jnp.concatenate([left, right], 1) + local_ref[...]
    out_ref[...] = total.astype(BF).reshape(out_ref.shape)


def finish_kernel(got_ref, own_ref, out_ref):
    out_ref.put((jnp.sum(got_ref[...].astype(F32), axis=0) + own_ref[...]).astype(BF))


def swap(values, axis):
    return lax.all_to_all(values, axis, split_axis=0, concat_axis=0, tiled=True)


def body(
    grid_latents,
    grid_region,
    grid_node,
    mesh_latents,
    edge_latents,
    edge_sender,
    edge_receiver,
    halo_send,
    w_grid,
    w_edge_in,
    w_edge_out,
    w_node_in,
    w_node_out,
    cot_mesh,
    cot_edges,
):
    spaces = lax.axis_size("space")
    feats = lax.axis_size("feat")
    nodes, width = mesh_latents.shape
    edges = edge_latents.shape[0]
    count = halo_send.shape[2]
    share = nodes // feats
    slots = spaces * 8
    back = width + width // 2
    region_row = grid_region.reshape(1, -1)
    node_row = grid_node.reshape(1, -1)
    sender = edge_sender.reshape(1, -1)
    receiver = edge_receiver.reshape(1, -1)
    halo_t = halo_send.transpose(2, 0, 1)
    wide = 2 * width + width // 2 + 128

    def own_start():
        return pl.multiple_of(lax.axis_index("feat") * share, share)

    (packed,) = call(
        pack_kernel,
        [Push((slots, wide), BF)],
        [
            Fetch(array)
            for array in (region_row, node_row, halo_t, mesh_latents, w_grid, grid_latents)
        ],
    )
    got = swap(packed.reshape(spaces, 8, wide), "space").reshape(slots, wide)
    base, sender_local = call(
        ready_kernel,
        [Push((edges, width), F32), Push((edges, width), BF)],
        [Fetch(array) for array in (sender, receiver, mesh_latents, edge_latents, w_edge_in)],
    )
    (
        sums,
        new_edges,
        slope,
        xhat,
        rstd,
        sender_held,
        receiver_held,
        w_mid,
        w_out,
        mesh_own,
        cot_own,
        node_in,
        node_out,
        edge_cot,
    ) = call(
        functools.partial(edge_forward_kernel, count=count),
        [
            ((feats, share, 2 * width), BF),
            Push((edges, width), BF),
            ((edges, width), F32),
            ((edges, width), F32),
            ((edges, 128), F32),
        ],
        [
            got,
            Fetch(sender, keep=True),
            Fetch(receiver, keep=True),
            Fetch(sender_local),
            Fetch(w_edge_in, rows=width, start=width, keep=True),
            Fetch(base),
            Fetch(w_edge_out, keep=True),
            Fetch(edge_latents),
            Fetch(mesh_latents, rows=share, start=own_start, keep=True, defer=True),
            Fetch(cot_mesh, rows=share, start=own_start, keep=True, defer=True),
            Fetch(w_node_in, keep=True, defer=True),
            Fetch(w_node_out, keep=True, defer=True),
            Fetch(cot_edges, keep=True, defer=True),
        ],
    )
    sums = swap(sums, "feat")
    spread, new_share, own, w_first, w_last = call(
        node_kernel,
        [((feats, share, width), BF), ((share, width), BF), Push((share, width), F32)],
        [
            sums,
            mesh_own,
            node_in,
            node_out,
            cot_own,
            Fetch(w_edge_in, rows=width, start=0, keep=True),
            Fetch(w_edge_in, rows=width, start=2 * width, keep=True),
        ],
    )
    grads = swap(spread, "feat").reshape(nodes, width)
    send, grad_edges, local, new_share = call(
        functools.partial(edge_back_kernel, count=count),
        [
            Push((slots, back), BF),
            Push((edges, width), BF),
            Push((nodes, width), F32),
            Push((share, width), BF),
        ],
        [
            grads,
            edge_cot,
            w_out,
            w_mid,
            sender_held,
            receiver_held,
            xhat,
            rstd,
            slope,
            w_first,
            w_last,
            new_share,
        ],
    )
    returned = swap(send.reshape(spaces, 8, back), "space").reshape(slots, back)
    new_mesh = lax.all_gather(new_share, "feat", axis=0, tiled=True)
    parts, new_mesh, own = call(
        return_kernel,
        [((feats, share, width), BF), Push((nodes, width), BF)],
        [
            returned,
            Fetch(halo_t),
            Fetch(local),
            Fetch(own, keep=True),
            new_mesh,
        ],
    )
    last = swap(parts, "feat")
    (grad_mesh,) = call(finish_kernel, [Push((share, width), BF)], [last, own])
    return new_mesh, new_edges, grad_mesh, grad_edges


def solution(mesh):
    return jax.shard_map(
        body,
        mesh=mesh,
        in_specs=(
            P(("space", "feat"), None),
            P(("space", "feat"), None),
            P(("space", "feat")),
            P("space", None),
            P(("space", "feat"), None),
            P(("space", "feat")),
            P(("space", "feat")),
            P("space", None, None),
            P(),
            P(),
            P(),
            P(),
            P(),
            P("space", None),
            P(("space", "feat"), None),
        ),
        out_specs=(
            P("space", None),
            P(("space", "feat"), None),
            P(("space", "feat"), None),
            P(("space", "feat"), None),
        ),
        check_vma=False,
    )
```

```python
import functools

import jax
import jax.numpy as jnp
from jax import lax
from jax.experimental import pallas as pl
from jax.experimental.pallas import tpu as pltpu
from jax.sharding import PartitionSpec as P

BF = jnp.bfloat16
F32 = jnp.float32
VMEM_BYTES = 20 * 1024 * 1024


def mm(a, b):
    return jnp.dot(a, b, preferred_element_type=F32)


def mm_nt(a, b):
    return lax.dot_general(a, b, (((1,), (1,)), ((), ())), preferred_element_type=F32)


def iota(shape, dim):
    return lax.broadcasted_iota(jnp.int32, shape, dim)


def one_hot(a, b):
    return (a == b).astype(F32).astype(BF)


def column_of(row):
    n = row.shape[1]
    eye = iota((n, n), 0) == iota((n, n), 1)
    return jnp.sum(jnp.where(eye, row.astype(F32), 0.0), axis=1, keepdims=True).astype(jnp.int32)


class Fetch:
    def __init__(self, array, rows=None, start=None, keep=False, defer=False):
        self.array, self.start, self.keep, self.defer = array, start, keep, defer
        self.shape = array.shape if rows is None else (rows,) + array.shape[1:]

    def source(self, ref):
        if self.start is None:
            return ref
        return ref.at[pl.ds(self.start() if callable(self.start) else self.start, self.shape[0])]


class Push:
    def __init__(self, shape, dtype):
        self.shape, self.dtype = shape, dtype


class Late:
    def __init__(self, source, target, sem, defer):
        self.ref, self.shape = target, target.shape
        self.started = self.waited = False
        self.copy = pltpu.make_async_copy(source, target, sem)
        if not defer:
            self.start()

    def start(self):
        if not self.started:
            self.copy.start()
            self.started = True

    def wait(self):
        self.start()
        if not self.waited:
            self.copy.wait()
            self.waited = True

    def __getitem__(self, index):
        self.wait()
        return self.ref[index]


class Out:
    def __init__(self, target, scratch, sems):
        self.target, self.ref, self.sems, self.copies = target, scratch, sems, []
        self.shape = scratch.shape

    def put(self, value, *columns):
        source, target = self.ref, self.target
        if columns:
            index = (slice(None),) * (len(self.shape) - 1) + (slice(*columns),)
            self.ref[index] = value
            source, target = source.at[index], target.at[index]
        else:
            self.ref[...] = value
        copy = pltpu.make_async_copy(source, target, next(self.sems))
        copy.start()
        self.copies.append(copy)

    def __setitem__(self, index, value):
        self.ref[index] = value

    def finish(self):
        if not self.copies:
            self.copies.append(pltpu.make_async_copy(self.ref, self.target, next(self.sems)))
            self.copies[0].start()

    def wait(self):
        for copy in self.copies:
            copy.wait()


def call(kernel, outs, args):
    fetches = [arg for arg in args if isinstance(arg, Fetch)]
    kept = [arg for arg in fetches if arg.keep]
    pushes = [out for out in outs if isinstance(out, Push)]
    semaphores = len(fetches) + 4 * len(pushes)

    def run(*refs):
        ins, refs = refs[: len(args)], refs[len(args) :]
        plain_outs, refs = refs[: len(outs)], refs[len(outs) :]
        kept_refs, refs = iter(refs[: len(kept)]), refs[len(kept) :]
        scratch = iter(refs)
        sems = iter([refs[-1].at[i] for i in range(semaphores)] if semaphores else [])
        given = []
        for arg, ref in zip(args, ins):
            if isinstance(arg, Fetch):
                target = next(kept_refs if arg.keep else scratch)
                ref = Late(arg.source(ref), target, next(sems), arg.defer)
            given.append(ref)
        for out, ref in zip(outs, plain_outs):
            given.append(Out(ref, next(scratch), sems) if isinstance(out, Push) else ref)
        kernel(*given)
        for ref in given:
            if isinstance(ref, Out):
                ref.finish()
        for ref in given:
            if isinstance(ref, (Late, Out)):
                ref.wait()

    vmem = pl.BlockSpec(memory_space=pltpu.VMEM)
    hbm = pl.BlockSpec(memory_space=pltpu.HBM)
    scratch = [pltpu.VMEM(arg.shape, arg.array.dtype) for arg in fetches if not arg.keep]
    scratch += [pltpu.VMEM(out.shape, out.dtype) for out in pushes]
    if semaphores:
        scratch.append(pltpu.SemaphoreType.DMA((semaphores,)))
    out_shape = [
        pltpu.HBM(out.shape, out.dtype) if isinstance(out, Push) else pltpu.VMEM(*out)
        for out in outs
    ]
    results = pl.pallas_call(
        run,
        out_shape=out_shape + [pltpu.VMEM(arg.shape, arg.array.dtype) for arg in kept],
        in_specs=[hbm if isinstance(arg, Fetch) else vmem for arg in args],
        out_specs=[hbm if isinstance(out, Push) else vmem for out in outs] + [vmem] * len(kept),
        scratch_shapes=scratch,
        compiler_params=pltpu.CompilerParams(vmem_limit_bytes=VMEM_BYTES),
    )(
        *[
            pltpu.with_memory_space_constraint(arg.array, pltpu.HBM)
            if isinstance(arg, Fetch)
            else arg
            for arg in args
        ]
    )
    return results


def halo_column(halo_t, block, offset):
    count, spaces = halo_t.shape
    rows = spaces * 8
    spread = one_hot(iota((rows, spaces), 0) // 8, iota((rows, spaces), 1))
    all_k = mm_nt(spread, halo_t.astype(F32).astype(BF))
    wanted = offset + (iota((rows, count), 0) % 8) % block
    keep = wanted == iota((rows, count), 1)
    return jnp.sum(jnp.where(keep, all_k, 0.0), axis=1, keepdims=True).astype(jnp.int32)


def halo_row(halo_t, block, offset):
    count, spaces = halo_t.shape
    rows = spaces * 8
    spread = one_hot(iota((spaces, rows), 0), iota((spaces, rows), 1) // 8)
    all_k = mm(halo_t.astype(F32).astype(BF), spread)
    wanted = offset + (iota((count, rows), 1) % 8) % block
    keep = wanted == iota((count, rows), 0)
    return jnp.sum(jnp.where(keep, all_k, 0.0), axis=0, keepdims=True).astype(jnp.int32)


def silu_parts(v):
    s = 1.0 / (1.0 + jnp.exp(-v))
    return v * s, s * (1.0 + v * (1.0 - s))


def pack_kernel(region_ref, node_ref, halo_ref, mesh_ref, w_ref, grid_ref, out_ref):
    rows, width = grid_ref.shape
    half = width // 2
    spaces = halo_ref.shape[2]
    slots = spaces * 8
    region = region_ref[...]
    member = one_hot(iota((spaces, rows), 0), region)
    before = (iota((rows, rows), 0) < iota((rows, rows), 1)).astype(F32).astype(BF)
    earlier = mm(member, before)
    rank = jnp.sum(earlier * member.astype(F32), axis=0, keepdims=True).astype(jnp.int32)
    place = iota((slots, rows), 0) == region * 8 + rank
    label = (node_ref[...] + 1).astype(F32)
    labels = jnp.sum(jnp.where(place, label, 0.0), axis=1, keepdims=True)
    wide = out_ref.shape[1]
    out_ref.put(jnp.broadcast_to(labels, (slots, 128)).astype(BF), 2 * width + half, wide)
    halo_t = halo_ref[...].reshape(halo_ref.shape[0], spaces)
    first = halo_column(halo_t, 8, 0)
    rest = halo_column(halo_t, 4, 8)
    mesh = mesh_ref[...]
    ids = iota((slots, mesh.shape[0]), 1)
    out_ref.put(mm(one_hot(first, ids), mesh).astype(BF), 0, width)
    tail = mm(one_hot(rest, ids), mesh)
    left = iota((slots, half), 0) % 8 < 4
    tail = jnp.where(left, tail[:, :half], tail[:, half:]).astype(BF)
    out_ref.put(tail, width, width + half)
    message = silu_parts(mm(grid_ref[...], w_ref[...]))[0].astype(BF)
    placed = mm(place.astype(F32).astype(BF), message).astype(BF)
    out_ref.put(placed, width + half, 2 * width + half)


def table_ids(shape, dim, nodes, count):
    index = iota(shape, dim)
    j = index % 8
    base = nodes + index // 8 * count
    tail = base + 8 + j % 4
    return base + j, jnp.where(j < 4, tail, -1), jnp.where(j < 4, -1, tail)


def ready_kernel(sender_ref, receiver_ref, mesh_ref, edge_ref, w_in_ref, base_ref, local_ref):
    edges, width = edge_ref.shape
    nodes = mesh_ref.shape[0]
    ids = iota((edges, nodes), 1)
    mesh = mesh_ref[...]
    receiver_rows = mm(one_hot(column_of(receiver_ref[...]), ids), mesh).astype(BF)
    local_ref.put(mm(one_hot(column_of(sender_ref[...]), ids), mesh).astype(BF))
    base = mm(edge_ref[...], w_in_ref[:width, :])
    base_ref.put(base + mm(receiver_rows, w_in_ref[2 * width :, :]))


def edge_forward_kernel(
    got_ref,
    sender_ref,
    receiver_ref,
    local_ref,
    w_mid_ref,
    base_ref,
    w_out_ref,
    edge_ref,
    w_grid_sum_ref,
    w_edge_sum_ref,
    mesh_ref,
    cot_ref,
    w_mesh_ref,
    node_out_ref,
    cot_edges_ref,
    w_first_ref,
    w_last_ref,
    sums_ref,
    new_ref,
    slope_ref,
    xhat_ref,
    rstd_ref,
    count,
):
    edges, width = edge_ref.shape
    half = width // 2
    slots = got_ref.shape[0]
    feats, share, _ = sums_ref.shape
    nodes = feats * share
    label = got_ref[:, 2 * width + half :].astype(F32).T[0:1, :].astype(jnp.int32)
    grid_sum = mm(
        one_hot(iota((nodes, slots), 0) + 1, label), got_ref[:, width + half : 2 * width + half]
    ).astype(BF)
    sender = column_of(sender_ref[...])
    whole, left, right = table_ids((1, slots), 1, nodes, count)
    head = mm(one_hot(sender, whole), got_ref[:, :width])
    tail = got_ref[:, width : width + half]
    tails = [mm(one_hot(sender, left), tail), mm(one_hot(sender, right), tail)]
    for later in (mesh_ref, cot_ref, w_mesh_ref, node_out_ref, cot_edges_ref):
        later.start()
    w_first_ref.start()
    w_last_ref.start()
    head = head + jnp.concatenate(tails, 1) + local_ref[...].astype(F32)
    v = mm(head.astype(BF), w_mid_ref[...]) + base_ref[...]
    act, slope = silu_parts(v)
    slope_ref[...] = slope
    u = mm(act.astype(BF), w_out_ref[...])
    center = u - jnp.mean(u, -1, keepdims=True)
    rstd = lax.rsqrt(jnp.mean(center * center, -1, keepdims=True) + 1e-05)
    xhat = center * rstd
    xhat_ref[...] = xhat
    rstd_ref[...] = jnp.broadcast_to(rstd, rstd_ref.shape)
    new = (edge_ref[...].astype(F32) + xhat).astype(BF)
    new_ref.put(new)
    to_receiver = one_hot(iota((nodes, edges), 0), receiver_ref[...])
    edge_sum = mm(to_receiver, new).astype(BF)
    terms = mm(grid_sum, w_grid_sum_ref[...]) + mm(edge_sum, w_edge_sum_ref[...])
    sums_ref[...] = terms.astype(BF).reshape(feats, share, width)


def node_kernel(
    sums_ref,
    mesh_ref,
    w_mesh_ref,
    w_edge_sum_ref,
    w_out_ref,
    cot_ref,
    spread_ref,
    new_ref,
    own_ref,
):
    mesh = mesh_ref[...]
    cot = cot_ref[...].astype(F32)
    v = mm(mesh, w_mesh_ref[...]) + jnp.sum(sums_ref[...].astype(F32), axis=0)
    act, slope = silu_parts(v)
    u = mm(act.astype(BF), w_out_ref[...])
    center = u - jnp.mean(u, -1, keepdims=True)
    rstd = lax.rsqrt(jnp.mean(center * center, -1, keepdims=True) + 1e-05)
    xhat = center * rstd
    new_ref[...] = (mesh.astype(F32) + xhat).astype(BF)
    du = norm_back(cot, xhat, rstd)
    dh = mm_nt(du.astype(BF), w_out_ref[...]).astype(BF)
    dv = (dh.astype(F32) * slope).astype(BF)
    sum_grad = mm_nt(dv, w_edge_sum_ref[...]).astype(BF)
    spread_ref[...] = jnp.broadcast_to(sum_grad[None], spread_ref.shape)
    own_ref[...] = cot + mm_nt(dv, w_mesh_ref[...]).astype(BF).astype(F32)


def norm_back(cot, xhat, rstd):
    return rstd * (
        cot
        - jnp.mean(cot, -1, keepdims=True)
        - xhat * jnp.mean(cot * xhat, -1, keepdims=True)
    )


def edge_back_kernel(
    grads_ref,
    cot_ref,
    w_out_ref,
    w_mid_ref,
    sender_ref,
    receiver_ref,
    xhat_ref,
    rstd_ref,
    slope_ref,
    w_first_ref,
    w_last_ref,
    new_ref,
    own_ref,
    send_ref,
    grad_ref,
    local_ref,
    new_again_ref,
    own_again_ref,
    count,
):
    new_again_ref.put(new_ref[...])
    own_again_ref.put(own_ref[...])
    edges, width = cot_ref.shape
    half = width // 2
    nodes = grads_ref.shape[0]
    slots = send_ref.shape[0]
    sender, receiver = sender_ref[...], receiver_ref[...]
    spread = mm(one_hot(column_of(receiver), iota((edges, nodes), 1)), grads_ref[...])
    cot = (cot_ref[...].astype(F32) + spread).astype(BF)
    du = norm_back(cot.astype(F32), xhat_ref[...], rstd_ref[:, 0:1])
    dh = mm_nt(du.astype(BF), w_out_ref[...]).astype(BF)
    dv = (dh.astype(F32) * slope_ref[...]).astype(BF)
    sgrad = mm_nt(dv, w_mid_ref[...]).astype(BF)
    whole, left, right = table_ids((slots, 1), 0, nodes, count)
    send_ref.put(mm(one_hot(whole, sender), sgrad).astype(BF), 0, width)
    tail = mm(one_hot(jnp.maximum(left, right), sender), sgrad)
    tail = jnp.where(left >= 0, tail[:, :half], tail[:, half:]).astype(BF)
    send_ref.put(tail, width, width + half)
    rgrad = mm_nt(dv, w_last_ref[...]).astype(BF)
    ids = iota((nodes, edges), 0)
    local_ref.put(mm(one_hot(ids, sender), sgrad) + mm(one_hot(ids, receiver), rgrad))
    direct = mm_nt(dv, w_first_ref[...]).astype(BF)
    grad_ref.put((cot.astype(F32) + direct.astype(F32)).astype(BF))


def return_kernel(got_ref, halo_ref, local_ref, own_ref, new_ref, out_ref, new_out_ref):
    new_out_ref.put(new_ref[...])
    nodes, width = local_ref.shape
    slots = got_ref.shape[0]
    halo_t = halo_ref[...].reshape(halo_ref.shape[0], slots // 8)
    ids = iota((nodes, slots), 0)
    total = mm(one_hot(ids, halo_row(halo_t, 8, 0)), got_ref[:, :width])
    rest = halo_row(halo_t, 4, 8)
    is_left = iota((1, slots), 1) % 8 < 4
    tail = got_ref[:, width:]
    left = mm(one_hot(ids, jnp.where(is_left, rest, -1)), tail)
    right = mm(one_hot(ids, jnp.where(is_left, -1, rest)), tail)
    total = total + jnp.concatenate([left, right], 1) + local_ref[...]
    out_ref[...] = total.astype(BF).reshape(out_ref.shape)


def finish_kernel(got_ref, own_ref, out_ref):
    out_ref.put((jnp.sum(got_ref[...].astype(F32), axis=0) + own_ref[...]).astype(BF))


def swap(values, axis):
    return lax.all_to_all(values, axis, split_axis=0, concat_axis=0, tiled=True)


def body(
    grid_latents,
    grid_region,
    grid_node,
    mesh_latents,
    edge_latents,
    edge_sender,
    edge_receiver,
    halo_send,
    w_grid,
    w_edge_in,
    w_edge_out,
    w_node_in,
    w_node_out,
    cot_mesh,
    cot_edges,
):
    spaces = lax.axis_size("space")
    feats = lax.axis_size("feat")
    nodes, width = mesh_latents.shape
    edges = edge_latents.shape[0]
    count = halo_send.shape[2]
    share = nodes // feats
    slots = spaces * 8
    back = width + width // 2
    region_row = grid_region.reshape(1, -1)
    node_row = grid_node.reshape(1, -1)
    sender = edge_sender.reshape(1, -1)
    receiver = edge_receiver.reshape(1, -1)
    halo_t = halo_send.transpose(2, 0, 1)
    wide = 2 * width + width // 2 + 128

    def own_start():
        return pl.multiple_of(lax.axis_index("feat") * share, share)

    (packed,) = call(
        pack_kernel,
        [Push((slots, wide), BF)],
        [
            Fetch(array)
            for array in (region_row, node_row, halo_t, mesh_latents, w_grid, grid_latents)
        ],
    )
    got = swap(packed.reshape(spaces, 8, wide), "space").reshape(slots, wide)
    base, sender_local = call(
        ready_kernel,
        [Push((edges, width), F32), Push((edges, width), BF)],
        [Fetch(array) for array in (sender, receiver, mesh_latents, edge_latents, w_edge_in)],
    )
    (
        sums,
        new_edges,
        slope,
        xhat,
        rstd,
        sender_held,
        receiver_held,
        w_mid,
        w_out,
        w_edge_sum,
        mesh_own,
        cot_own,
        w_mesh,
        node_out,
        edge_cot,
        w_first,
        w_last,
    ) = call(
        functools.partial(edge_forward_kernel, count=count),
        [
            ((feats, share, width), BF),
            Push((edges, width), BF),
            ((edges, width), F32),
            ((edges, width), F32),
            ((edges, 128), F32),
        ],
        [
            got,
            Fetch(sender, keep=True),
            Fetch(receiver, keep=True),
            Fetch(sender_local),
            Fetch(w_edge_in, rows=width, start=width, keep=True),
            Fetch(base),
            Fetch(w_edge_out, keep=True),
            Fetch(edge_latents),
            Fetch(w_node_in, rows=width, start=width),
            Fetch(w_node_in, rows=width, start=2 * width, keep=True),
            Fetch(mesh_latents, rows=share, start=own_start, keep=True, defer=True),
            Fetch(cot_mesh, rows=share, start=own_start, keep=True, defer=True),
            Fetch(w_node_in, rows=width, start=0, keep=True, defer=True),
            Fetch(w_node_out, keep=True, defer=True),
            Fetch(cot_edges, keep=True, defer=True),
            Fetch(w_edge_in, rows=width, start=0, keep=True, defer=True),
            Fetch(w_edge_in, rows=width, start=2 * width, keep=True, defer=True),
        ],
    )
    sums = swap(sums, "feat")
    spread, new_share, own = call(
        node_kernel,
        [((feats, share, width), BF), ((share, width), BF), ((share, width), F32)],
        [sums, mesh_own, w_mesh, w_edge_sum, node_out, cot_own],
    )
    grads = swap(spread, "feat").reshape(nodes, width)
    send, grad_edges, local, new_share, own = call(
        functools.partial(edge_back_kernel, count=count),
        [
            Push((slots, back), BF),
            Push((edges, width), BF),
            Push((nodes, width), F32),
            Push((share, width), BF),
            Push((share, width), F32),
        ],
        [
            grads,
            edge_cot,
            w_out,
            w_mid,
            sender_held,
            receiver_held,
            xhat,
            rstd,
            slope,
            w_first,
            w_last,
            new_share,
            own,
        ],
    )
    returned = swap(send.reshape(spaces, 8, back), "space").reshape(slots, back)
    new_mesh = lax.all_gather(new_share, "feat", axis=0, tiled=True)
    parts, new_mesh, own = call(
        return_kernel,
        [((feats, share, width), BF), Push((nodes, width), BF)],
        [
            returned,
            Fetch(halo_t),
            Fetch(local),
            Fetch(own, keep=True),
            new_mesh,
        ],
    )
    last = swap(parts, "feat")
    (grad_mesh,) = call(finish_kernel, [Push((share, width), BF)], [last, own])
    return new_mesh, new_edges, grad_mesh, grad_edges


def solution(mesh):
    return jax.shard_map(
        body,
        mesh=mesh,
        in_specs=(
            P(("space", "feat"), None),
            P(("space", "feat"), None),
            P(("space", "feat")),
            P("space", None),
            P(("space", "feat"), None),
            P(("space", "feat")),
            P(("space", "feat")),
            P("space", None, None),
            P(),
            P(),
            P(),
            P(),
            P(),
            P("space", None),
            P(("space", "feat"), None),
        ),
        out_specs=(
            P("space", None),
            P(("space", "feat"), None),
            P(("space", "feat"), None),
            P(("space", "feat"), None),
        ),
        check_vma=False,
    )
```

```python
import functools

import jax
import jax.numpy as jnp
from jax import lax
from jax.experimental import pallas as pl
from jax.experimental.pallas import tpu as pltpu
from jax.sharding import PartitionSpec as P

BF = jnp.bfloat16
F32 = jnp.float32
VMEM_BYTES = 20 * 1024 * 1024


def mm(a, b):
    return jnp.dot(a, b, preferred_element_type=F32)


def mm_nt(a, b):
    return lax.dot_general(a, b, (((1,), (1,)), ((), ())), preferred_element_type=F32)


def iota(shape, dim):
    return lax.broadcasted_iota(jnp.int32, shape, dim)


def one_hot(a, b):
    return (a == b).astype(F32).astype(BF)


def column_of(row):
    n = row.shape[1]
    eye = iota((n, n), 0) == iota((n, n), 1)
    return jnp.sum(jnp.where(eye, row.astype(F32), 0.0), axis=1, keepdims=True).astype(jnp.int32)


class Fetch:
    def __init__(self, array, rows=None, start=None, keep=False, defer=False):
        self.array, self.start, self.keep, self.defer = array, start, keep, defer
        self.shape = array.shape if rows is None else (rows,) + array.shape[1:]

    def source(self, ref):
        if self.start is None:
            return ref
        return ref.at[pl.ds(self.start() if callable(self.start) else self.start, self.shape[0])]


class Push:
    def __init__(self, shape, dtype):
        self.shape, self.dtype = shape, dtype


class Late:
    def __init__(self, source, target, sem, defer):
        self.ref, self.shape = target, target.shape
        self.started = self.waited = False
        self.copy = pltpu.make_async_copy(source, target, sem)
        if not defer:
            self.start()

    def start(self):
        if not self.started:
            self.copy.start()
            self.started = True

    def wait(self):
        self.start()
        if not self.waited:
            self.copy.wait()
            self.waited = True

    def __getitem__(self, index):
        self.wait()
        return self.ref[index]


class Out:
    def __init__(self, target, scratch, sems):
        self.target, self.ref, self.sems, self.copies = target, scratch, sems, []
        self.shape = scratch.shape

    def put(self, value, *columns):
        source, target = self.ref, self.target
        if columns:
            index = (slice(None),) * (len(self.shape) - 1) + (slice(*columns),)
            self.ref[index] = value
            source, target = source.at[index], target.at[index]
        else:
            self.ref[...] = value
        copy = pltpu.make_async_copy(source, target, next(self.sems))
        copy.start()
        self.copies.append(copy)

    def __setitem__(self, index, value):
        self.ref[index] = value

    def finish(self):
        if not self.copies:
            self.copies.append(pltpu.make_async_copy(self.ref, self.target, next(self.sems)))
            self.copies[0].start()

    def wait(self):
        for copy in self.copies:
            copy.wait()


def call(kernel, outs, args):
    fetches = [arg for arg in args if isinstance(arg, Fetch)]
    kept = [arg for arg in fetches if arg.keep]
    pushes = [out for out in outs if isinstance(out, Push)]
    semaphores = len(fetches) + 4 * len(pushes)

    def run(*refs):
        ins, refs = refs[: len(args)], refs[len(args) :]
        plain_outs, refs = refs[: len(outs)], refs[len(outs) :]
        kept_refs, refs = iter(refs[: len(kept)]), refs[len(kept) :]
        scratch = iter(refs)
        sems = iter([refs[-1].at[i] for i in range(semaphores)] if semaphores else [])
        given = []
        for arg, ref in zip(args, ins):
            if isinstance(arg, Fetch):
                target = next(kept_refs if arg.keep else scratch)
                ref = Late(arg.source(ref), target, next(sems), arg.defer)
            given.append(ref)
        for out, ref in zip(outs, plain_outs):
            given.append(Out(ref, next(scratch), sems) if isinstance(out, Push) else ref)
        kernel(*given)
        for ref in given:
            if isinstance(ref, Out):
                ref.finish()
        for ref in given:
            if isinstance(ref, (Late, Out)):
                ref.wait()

    vmem = pl.BlockSpec(memory_space=pltpu.VMEM)
    hbm = pl.BlockSpec(memory_space=pltpu.HBM)
    scratch = [pltpu.VMEM(arg.shape, arg.array.dtype) for arg in fetches if not arg.keep]
    scratch += [pltpu.VMEM(out.shape, out.dtype) for out in pushes]
    if semaphores:
        scratch.append(pltpu.SemaphoreType.DMA((semaphores,)))
    out_shape = [
        pltpu.HBM(out.shape, out.dtype) if isinstance(out, Push) else pltpu.VMEM(*out)
        for out in outs
    ]
    results = pl.pallas_call(
        run,
        out_shape=out_shape + [pltpu.VMEM(arg.shape, arg.array.dtype) for arg in kept],
        in_specs=[hbm if isinstance(arg, Fetch) else vmem for arg in args],
        out_specs=[hbm if isinstance(out, Push) else vmem for out in outs] + [vmem] * len(kept),
        scratch_shapes=scratch,
        compiler_params=pltpu.CompilerParams(vmem_limit_bytes=VMEM_BYTES),
    )(
        *[
            pltpu.with_memory_space_constraint(arg.array, pltpu.HBM)
            if isinstance(arg, Fetch)
            else arg
            for arg in args
        ]
    )
    return results


def halo_column(halo_t, block, offset):
    count, spaces = halo_t.shape
    rows = spaces * 8
    spread = one_hot(iota((rows, spaces), 0) // 8, iota((rows, spaces), 1))
    all_k = mm_nt(spread, halo_t.astype(F32).astype(BF))
    wanted = offset + (iota((rows, count), 0) % 8) % block
    keep = wanted == iota((rows, count), 1)
    return jnp.sum(jnp.where(keep, all_k, 0.0), axis=1, keepdims=True).astype(jnp.int32)


def halo_row(halo_t, block, offset):
    count, spaces = halo_t.shape
    rows = spaces * 8
    spread = one_hot(iota((spaces, rows), 0), iota((spaces, rows), 1) // 8)
    all_k = mm(halo_t.astype(F32).astype(BF), spread)
    wanted = offset + (iota((count, rows), 1) % 8) % block
    keep = wanted == iota((count, rows), 0)
    return jnp.sum(jnp.where(keep, all_k, 0.0), axis=0, keepdims=True).astype(jnp.int32)


def silu_parts(v):
    s = 1.0 / (1.0 + jnp.exp(-v))
    return v * s, s * (1.0 + v * (1.0 - s))


def pack_kernel(
    region_ref,
    node_ref,
    halo_ref,
    mesh_ref,
    w_ref,
    grid_ref,
    sender_ref,
    receiver_ref,
    edge_ref,
    w_in_ref,
    w_out_ref,
    w_sums_ref,
    out_ref,
):
    rows, width = grid_ref.shape
    half = width // 2
    spaces = halo_ref.shape[2]
    slots = spaces * 8
    region = region_ref[...]
    member = one_hot(iota((spaces, rows), 0), region)
    before = (iota((rows, rows), 0) < iota((rows, rows), 1)).astype(F32).astype(BF)
    earlier = mm(member, before)
    rank = jnp.sum(earlier * member.astype(F32), axis=0, keepdims=True).astype(jnp.int32)
    place = iota((slots, rows), 0) == region * 8 + rank
    label = (node_ref[...] + 1).astype(F32)
    labels = jnp.sum(jnp.where(place, label, 0.0), axis=1, keepdims=True)
    out_ref[:, 2 * width + half :] = jnp.broadcast_to(labels, (slots, 128)).astype(BF)
    halo_t = halo_ref[...].reshape(halo_ref.shape[0], spaces)
    first = halo_column(halo_t, 8, 0)
    rest = halo_column(halo_t, 4, 8)
    mesh = mesh_ref[...]
    ids = iota((slots, mesh.shape[0]), 1)
    out_ref[:, :width] = mm(one_hot(first, ids), mesh).astype(BF)
    tail = mm(one_hot(rest, ids), mesh)
    left = iota((slots, half), 0) % 8 < 4
    tail = jnp.where(left, tail[:, :half], tail[:, half:]).astype(BF)
    out_ref[:, width : width + half] = tail
    message = silu_parts(mm(grid_ref[...], w_ref[...]))[0].astype(BF)
    placed = mm(place.astype(F32).astype(BF), message).astype(BF)
    out_ref[:, width + half : 2 * width + half] = placed


def table_ids(shape, dim, nodes, count):
    index = iota(shape, dim)
    j = index % 8
    base = nodes + index // 8 * count
    tail = base + 8 + j % 4
    return base + j, jnp.where(j < 4, tail, -1), jnp.where(j < 4, -1, tail)


def edge_forward_kernel(
    got_ref,
    sender_ref,
    receiver_ref,
    mesh_ref,
    w_in_ref,
    w_out_ref,
    edge_ref,
    w_sums_ref,
    mesh_own_ref,
    cot_ref,
    w_mesh_ref,
    node_out_ref,
    cot_edges_ref,
    sums_ref,
    new_ref,
    slope_ref,
    xhat_ref,
    rstd_ref,
    count,
):
    edges, width = edge_ref.shape
    half = width // 2
    slots = got_ref.shape[0]
    feats, share, _ = sums_ref.shape
    nodes = feats * share
    receiver_row = receiver_ref[...].reshape(1, edges)
    sender = column_of(sender_ref[...].reshape(1, edges))
    whole, left, right = table_ids((1, slots), 1, nodes, count)
    mesh = mesh_ref[...]
    ids = iota((edges, nodes), 1)
    receiver_rows = mm(one_hot(column_of(receiver_row), ids), mesh).astype(BF)
    head = mm(one_hot(sender, whole), got_ref[:, :width])
    tail = got_ref[:, width : width + half]
    tails = [mm(one_hot(sender, left), tail), mm(one_hot(sender, right), tail)]
    head = head + jnp.concatenate(tails, 1) + mm(one_hot(sender, ids), mesh)
    v = mm(edge_ref[...], w_in_ref[:width, :]) + mm(receiver_rows, w_in_ref[2 * width :, :])
    v = v + mm(head.astype(BF), w_in_ref[width : 2 * width, :])
    act, slope = silu_parts(v)
    slope_ref[...] = slope
    u = mm(act.astype(BF), w_out_ref[...])
    center = u - jnp.mean(u, -1, keepdims=True)
    rstd = lax.rsqrt(jnp.mean(center * center, -1, keepdims=True) + 1e-05)
    xhat = center * rstd
    xhat_ref[...] = xhat
    rstd_ref[...] = jnp.broadcast_to(rstd, rstd_ref.shape)
    new = (edge_ref[...].astype(F32) + xhat).astype(BF)
    new_ref.put(new)
    to_receiver = one_hot(iota((nodes, edges), 0), receiver_row)
    label = got_ref[:, 2 * width + half :].astype(F32).T[0:1, :].astype(jnp.int32)
    grid_sum = mm(
        one_hot(iota((nodes, slots), 0) + 1, label), got_ref[:, width + half : 2 * width + half]
    ).astype(BF)
    edge_sum = mm(to_receiver, new).astype(BF)
    terms = mm(grid_sum, w_sums_ref[:width, :]) + mm(edge_sum, w_sums_ref[width:, :])
    sums_ref[...] = terms.astype(BF).reshape(feats, share, width)


def node_kernel(
    sums_ref,
    mesh_ref,
    w_mesh_ref,
    w_sums_ref,
    w_out_ref,
    cot_ref,
    spread_ref,
    new_ref,
    own_ref,
):
    mesh = mesh_ref[...]
    cot = cot_ref[...].astype(F32)
    v = mm(mesh, w_mesh_ref[...]) + jnp.sum(sums_ref[...].astype(F32), axis=0)
    act, slope = silu_parts(v)
    u = mm(act.astype(BF), w_out_ref[...])
    center = u - jnp.mean(u, -1, keepdims=True)
    rstd = lax.rsqrt(jnp.mean(center * center, -1, keepdims=True) + 1e-05)
    xhat = center * rstd
    new_ref[...] = (mesh.astype(F32) + xhat).astype(BF)
    du = norm_back(cot, xhat, rstd)
    dh = mm_nt(du.astype(BF), w_out_ref[...]).astype(BF)
    dv = (dh.astype(F32) * slope).astype(BF)
    sum_grad = mm_nt(dv, w_sums_ref[w_out_ref.shape[0] :, :]).astype(BF)
    spread_ref[...] = jnp.broadcast_to(sum_grad[None], spread_ref.shape)
    own_ref[...] = cot + mm_nt(dv, w_mesh_ref[...]).astype(BF).astype(F32)


def norm_back(cot, xhat, rstd):
    return rstd * (
        cot
        - jnp.mean(cot, -1, keepdims=True)
        - xhat * jnp.mean(cot * xhat, -1, keepdims=True)
    )


def edge_back_kernel(
    grads_ref,
    cot_ref,
    w_out_ref,
    w_in_ref,
    sender_ref,
    receiver_ref,
    xhat_ref,
    rstd_ref,
    slope_ref,
    new_ref,
    own_ref,
    send_ref,
    grad_ref,
    local_ref,
    new_again_ref,
    own_again_ref,
    count,
):
    new_again_ref.put(new_ref[...])
    own_again_ref.put(own_ref[...])
    edges, width = cot_ref.shape
    half = width // 2
    nodes = grads_ref.shape[0]
    slots = send_ref.shape[0]
    sender = sender_ref[...].reshape(1, edges)
    receiver = receiver_ref[...].reshape(1, edges)
    spread = mm(one_hot(column_of(receiver), iota((edges, nodes), 1)), grads_ref[...])
    cot = (cot_ref[...].astype(F32) + spread).astype(BF)
    du = norm_back(cot.astype(F32), xhat_ref[...], rstd_ref[:, 0:1])
    dh = mm_nt(du.astype(BF), w_out_ref[...]).astype(BF)
    dv = (dh.astype(F32) * slope_ref[...]).astype(BF)
    sgrad = mm_nt(dv, w_in_ref[width : 2 * width, :]).astype(BF)
    whole, left, right = table_ids((slots, 1), 0, nodes, count)
    send_ref.put(mm(one_hot(whole, sender), sgrad).astype(BF), 0, width)
    tail = mm(one_hot(jnp.maximum(left, right), sender), sgrad)
    tail = jnp.where(left >= 0, tail[:, :half], tail[:, half:]).astype(BF)
    send_ref.put(tail, width, width + half)
    rgrad = mm_nt(dv, w_in_ref[2 * width :, :]).astype(BF)
    ids = iota((nodes, edges), 0)
    local_ref.put(mm(one_hot(ids, sender), sgrad) + mm(one_hot(ids, receiver), rgrad))
    direct = mm_nt(dv, w_in_ref[:width, :]).astype(BF)
    grad_ref.put((cot.astype(F32) + direct.astype(F32)).astype(BF))


def return_kernel(got_ref, halo_ref, local_ref, own_ref, new_ref, out_ref, new_out_ref):
    new_out_ref.put(new_ref[...])
    nodes, width = local_ref.shape
    slots = got_ref.shape[0]
    halo_t = halo_ref[...].reshape(halo_ref.shape[0], slots // 8)
    ids = iota((nodes, slots), 0)
    total = mm(one_hot(ids, halo_row(halo_t, 8, 0)), got_ref[:, :width])
    rest = halo_row(halo_t, 4, 8)
    is_left = iota((1, slots), 1) % 8 < 4
    tail = got_ref[:, width:]
    left = mm(one_hot(ids, jnp.where(is_left, rest, -1)), tail)
    right = mm(one_hot(ids, jnp.where(is_left, -1, rest)), tail)
    total = total + jnp.concatenate([left, right], 1) + local_ref[...]
    out_ref[...] = total.astype(BF).reshape(out_ref.shape)


def finish_kernel(got_ref, own_ref, out_ref):
    out_ref.put((jnp.sum(got_ref[...].astype(F32), axis=0) + own_ref[...]).astype(BF))


def swap(values, axis):
    return lax.all_to_all(values, axis, split_axis=0, concat_axis=0, tiled=True)


def body(
    grid_latents,
    grid_region,
    grid_node,
    mesh_latents,
    edge_latents,
    edge_sender,
    edge_receiver,
    halo_send,
    w_grid,
    w_edge_in,
    w_edge_out,
    w_node_in,
    w_node_out,
    cot_mesh,
    cot_edges,
):
    spaces = lax.axis_size("space")
    feats = lax.axis_size("feat")
    nodes, width = mesh_latents.shape
    edges = edge_latents.shape[0]
    count = halo_send.shape[2]
    share = nodes // feats
    slots = spaces * 8
    back = width + width // 2
    region_row = grid_region.reshape(1, -1)
    node_row = grid_node.reshape(1, -1)
    halo_t = halo_send.transpose(2, 0, 1)
    wide = 2 * width + width // 2 + 128

    def own_start():
        return pl.multiple_of(lax.axis_index("feat") * share, share)

    packed, mesh, sender, receiver, edge, w_in, w_out, w_sums = call(
        pack_kernel,
        [((slots, wide), BF)],
        [
            Fetch(region_row),
            Fetch(node_row),
            Fetch(halo_t),
            Fetch(mesh_latents, keep=True),
            Fetch(w_grid),
            Fetch(grid_latents),
            Fetch(edge_sender, keep=True),
            Fetch(edge_receiver, keep=True),
            Fetch(edge_latents, keep=True),
            Fetch(w_edge_in, keep=True),
            Fetch(w_edge_out, keep=True),
            Fetch(w_node_in, rows=2 * width, start=width, keep=True),
        ],
    )
    got = swap(packed.reshape(spaces, 8, wide), "space").reshape(slots, wide)
    (
        sums,
        new_edges,
        slope,
        xhat,
        rstd,
        mesh_own,
        cot_own,
        w_mesh,
        node_out,
        edge_cot,
    ) = call(
        functools.partial(edge_forward_kernel, count=count),
        [
            ((feats, share, width), BF),
            Push((edges, width), BF),
            ((edges, width), F32),
            ((edges, width), F32),
            ((edges, 128), F32),
        ],
        [
            got,
            sender,
            receiver,
            mesh,
            w_in,
            w_out,
            edge,
            w_sums,
            Fetch(mesh_latents, rows=share, start=own_start, keep=True),
            Fetch(cot_mesh, rows=share, start=own_start, keep=True),
            Fetch(w_node_in, rows=width, start=0, keep=True),
            Fetch(w_node_out, keep=True),
            Fetch(cot_edges, keep=True),
        ],
    )
    sums = swap(sums, "feat")
    spread, new_share, own = call(
        node_kernel,
        [((feats, share, width), BF), ((share, width), BF), ((share, width), F32)],
        [sums, mesh_own, w_mesh, w_sums, node_out, cot_own],
    )
    grads = swap(spread, "feat").reshape(nodes, width)
    send, grad_edges, local, new_share, own = call(
        functools.partial(edge_back_kernel, count=count),
        [
            Push((slots, back), BF),
            Push((edges, width), BF),
            Push((nodes, width), F32),
            Push((share, width), BF),
            Push((share, width), F32),
        ],
        [
            grads,
            edge_cot,
            w_out,
            w_in,
            sender,
            receiver,
            xhat,
            rstd,
            slope,
            new_share,
            own,
        ],
    )
    returned = swap(send.reshape(spaces, 8, back), "space").reshape(slots, back)
    new_mesh = lax.all_gather(new_share, "feat", axis=0, tiled=True)
    parts, new_mesh, own = call(
        return_kernel,
        [((feats, share, width), BF), Push((nodes, width), BF)],
        [
            returned,
            Fetch(halo_t),
            Fetch(local),
            Fetch(own, keep=True),
            new_mesh,
        ],
    )
    last = swap(parts, "feat")
    (grad_mesh,) = call(finish_kernel, [Push((share, width), BF)], [last, own])
    return new_mesh, new_edges, grad_mesh, grad_edges


def solution(mesh):
    return jax.shard_map(
        body,
        mesh=mesh,
        in_specs=(
            P(("space", "feat"), None),
            P(("space", "feat"), None),
            P(("space", "feat")),
            P("space", None),
            P(("space", "feat"), None),
            P(("space", "feat")),
            P(("space", "feat")),
            P("space", None, None),
            P(),
            P(),
            P(),
            P(),
            P(),
            P("space", None),
            P(("space", "feat"), None),
        ),
        out_specs=(
            P("space", None),
            P(("space", "feat"), None),
            P(("space", "feat"), None),
            P(("space", "feat"), None),
        ),
        check_vma=False,
    )
```

```python
import functools

import jax
import jax.numpy as jnp
from jax import lax
from jax.experimental import pallas as pl
from jax.experimental.pallas import tpu as pltpu
from jax.sharding import PartitionSpec as P

BF = jnp.bfloat16
F32 = jnp.float32
VMEM_BYTES = 20 * 1024 * 1024


def mm(a, b):
    return jnp.dot(a, b, preferred_element_type=F32)


def mm_nt(a, b):
    return lax.dot_general(a, b, (((1,), (1,)), ((), ())), preferred_element_type=F32)


def iota(shape, dim):
    return lax.broadcasted_iota(jnp.int32, shape, dim)


def one_hot(a, b):
    return (a == b).astype(F32).astype(BF)


def column_of(row):
    n = row.shape[1]
    eye = iota((n, n), 0) == iota((n, n), 1)
    return jnp.sum(jnp.where(eye, row.astype(F32), 0.0), axis=1, keepdims=True).astype(jnp.int32)


class Fetch:
    def __init__(self, array, rows=None, start=None, keep=False, defer=False):
        self.array, self.start, self.keep, self.defer = array, start, keep, defer
        self.shape = array.shape if rows is None else (rows,) + array.shape[1:]

    def source(self, ref):
        if self.start is None:
            return ref
        return ref.at[pl.ds(self.start() if callable(self.start) else self.start, self.shape[0])]


class Push:
    def __init__(self, shape, dtype):
        self.shape, self.dtype = shape, dtype


class Late:
    def __init__(self, source, target, sem, defer):
        self.ref, self.shape = target, target.shape
        self.started = self.waited = False
        self.copy = pltpu.make_async_copy(source, target, sem)
        if not defer:
            self.start()

    def start(self):
        if not self.started:
            self.copy.start()
            self.started = True

    def wait(self):
        self.start()
        if not self.waited:
            self.copy.wait()
            self.waited = True

    def __getitem__(self, index):
        self.wait()
        return self.ref[index]


class Out:
    def __init__(self, target, scratch, sems):
        self.target, self.ref, self.sems, self.copies = target, scratch, sems, []
        self.shape = scratch.shape

    def put(self, value, *columns):
        source, target = self.ref, self.target
        if columns:
            index = (slice(None),) * (len(self.shape) - 1) + (slice(*columns),)
            self.ref[index] = value
            source, target = source.at[index], target.at[index]
        else:
            self.ref[...] = value
        copy = pltpu.make_async_copy(source, target, next(self.sems))
        copy.start()
        self.copies.append(copy)

    def __setitem__(self, index, value):
        self.ref[index] = value

    def finish(self):
        if not self.copies:
            self.copies.append(pltpu.make_async_copy(self.ref, self.target, next(self.sems)))
            self.copies[0].start()

    def wait(self):
        for copy in self.copies:
            copy.wait()


def call(kernel, outs, args):
    fetches = [arg for arg in args if isinstance(arg, Fetch)]
    kept = [arg for arg in fetches if arg.keep]
    pushes = [out for out in outs if isinstance(out, Push)]
    semaphores = len(fetches) + 4 * len(pushes)

    def run(*refs):
        ins, refs = refs[: len(args)], refs[len(args) :]
        plain_outs, refs = refs[: len(outs)], refs[len(outs) :]
        kept_refs, refs = iter(refs[: len(kept)]), refs[len(kept) :]
        scratch = iter(refs)
        sems = iter([refs[-1].at[i] for i in range(semaphores)] if semaphores else [])
        given = []
        for arg, ref in zip(args, ins):
            if isinstance(arg, Fetch):
                target = next(kept_refs if arg.keep else scratch)
                ref = Late(arg.source(ref), target, next(sems), arg.defer)
            given.append(ref)
        for out, ref in zip(outs, plain_outs):
            given.append(Out(ref, next(scratch), sems) if isinstance(out, Push) else ref)
        kernel(*given)
        for ref in given:
            if isinstance(ref, Out):
                ref.finish()
        for ref in given:
            if isinstance(ref, (Late, Out)):
                ref.wait()

    vmem = pl.BlockSpec(memory_space=pltpu.VMEM)
    hbm = pl.BlockSpec(memory_space=pltpu.HBM)
    scratch = [pltpu.VMEM(arg.shape, arg.array.dtype) for arg in fetches if not arg.keep]
    scratch += [pltpu.VMEM(out.shape, out.dtype) for out in pushes]
    if semaphores:
        scratch.append(pltpu.SemaphoreType.DMA((semaphores,)))
    out_shape = [
        pltpu.HBM(out.shape, out.dtype) if isinstance(out, Push) else pltpu.VMEM(*out)
        for out in outs
    ]
    results = pl.pallas_call(
        run,
        out_shape=out_shape + [pltpu.VMEM(arg.shape, arg.array.dtype) for arg in kept],
        in_specs=[hbm if isinstance(arg, Fetch) else vmem for arg in args],
        out_specs=[hbm if isinstance(out, Push) else vmem for out in outs] + [vmem] * len(kept),
        scratch_shapes=scratch,
        compiler_params=pltpu.CompilerParams(vmem_limit_bytes=VMEM_BYTES),
    )(
        *[
            pltpu.with_memory_space_constraint(arg.array, pltpu.HBM)
            if isinstance(arg, Fetch)
            else arg
            for arg in args
        ]
    )
    return results


def halo_column(halo_t, block, offset):
    count, spaces = halo_t.shape
    rows = spaces * 8
    spread = one_hot(iota((rows, spaces), 0) // 8, iota((rows, spaces), 1))
    all_k = mm_nt(spread, halo_t.astype(F32).astype(BF))
    wanted = offset + (iota((rows, count), 0) % 8) % block
    keep = wanted == iota((rows, count), 1)
    return jnp.sum(jnp.where(keep, all_k, 0.0), axis=1, keepdims=True).astype(jnp.int32)


def halo_row(halo_t, block, offset):
    count, spaces = halo_t.shape
    rows = spaces * 8
    spread = one_hot(iota((spaces, rows), 0), iota((spaces, rows), 1) // 8)
    all_k = mm(halo_t.astype(F32).astype(BF), spread)
    wanted = offset + (iota((count, rows), 1) % 8) % block
    keep = wanted == iota((count, rows), 0)
    return jnp.sum(jnp.where(keep, all_k, 0.0), axis=0, keepdims=True).astype(jnp.int32)


def silu_parts(v):
    s = 1.0 / (1.0 + jnp.exp(-v))
    return v * s, s * (1.0 + v * (1.0 - s))


def pack_kernel(region_ref, node_ref, halo_ref, mesh_ref, w_ref, grid_ref, out_ref):
    rows, width = grid_ref.shape
    half = width // 2
    spaces = halo_ref.shape[2]
    slots = spaces * 8
    region = region_ref[...]
    member = one_hot(iota((spaces, rows), 0), region)
    before = (iota((rows, rows), 0) < iota((rows, rows), 1)).astype(F32).astype(BF)
    earlier = mm(member, before)
    rank = jnp.sum(earlier * member.astype(F32), axis=0, keepdims=True).astype(jnp.int32)
    place = iota((slots, rows), 0) == region * 8 + rank
    label = (node_ref[...] + 1).astype(F32)
    labels = jnp.sum(jnp.where(place, label, 0.0), axis=1, keepdims=True)
    wide = out_ref.shape[1]
    out_ref.put(jnp.broadcast_to(labels, (slots, 128)).astype(BF), 2 * width + half, wide)
    halo_t = halo_ref[...].reshape(halo_ref.shape[0], spaces)
    first = halo_column(halo_t, 8, 0)
    rest = halo_column(halo_t, 4, 8)
    mesh = mesh_ref[...]
    ids = iota((slots, mesh.shape[0]), 1)
    out_ref.put(mm(one_hot(first, ids), mesh).astype(BF), 0, width)
    tail = mm(one_hot(rest, ids), mesh)
    left = iota((slots, half), 0) % 8 < 4
    tail = jnp.where(left, tail[:, :half], tail[:, half:]).astype(BF)
    out_ref.put(tail, width, width + half)
    message = silu_parts(mm(grid_ref[...], w_ref[...]))[0].astype(BF)
    placed = mm(place.astype(F32).astype(BF), message).astype(BF)
    out_ref.put(placed, width + half, 2 * width + half)


def table_ids(shape, dim, nodes, count):
    index = iota(shape, dim)
    j = index % 8
    base = nodes + index // 8 * count
    tail = base + 8 + j % 4
    return base + j, jnp.where(j < 4, tail, -1), jnp.where(j < 4, -1, tail)


def ready_kernel(sender_ref, receiver_ref, mesh_ref, edge_ref, w_in_ref, base_ref, local_ref):
    edges, width = edge_ref.shape
    nodes = mesh_ref.shape[0]
    ids = iota((edges, nodes), 1)
    mesh = mesh_ref[...]
    receiver_rows = mm(one_hot(column_of(receiver_ref[...]), ids), mesh).astype(BF)
    local_ref.put(mm(one_hot(column_of(sender_ref[...]), ids), mesh).astype(BF))
    base = mm(edge_ref[...], w_in_ref[:width, :])
    base_ref.put(base + mm(receiver_rows, w_in_ref[2 * width :, :]))


def edge_forward_kernel(
    got_ref,
    sender_ref,
    receiver_ref,
    local_ref,
    w_mid_ref,
    base_ref,
    w_out_ref,
    edge_ref,
    w_grid_sum_ref,
    w_edge_sum_ref,
    mesh_ref,
    cot_ref,
    w_mesh_ref,
    node_out_ref,
    cot_edges_ref,
    w_first_ref,
    w_last_ref,
    sums_ref,
    new_ref,
    slope_ref,
    xhat_ref,
    rstd_ref,
    count,
):
    edges, width = edge_ref.shape
    half = width // 2
    slots = got_ref.shape[0]
    feats, share, _ = sums_ref.shape
    nodes = feats * share
    label = got_ref[:, 2 * width + half :].astype(F32).T[0:1, :].astype(jnp.int32)
    grid_sum = mm(
        one_hot(iota((nodes, slots), 0) + 1, label), got_ref[:, width + half : 2 * width + half]
    ).astype(BF)
    sender = column_of(sender_ref[...])
    whole, left, right = table_ids((1, slots), 1, nodes, count)
    head = mm(one_hot(sender, whole), got_ref[:, :width])
    tail = got_ref[:, width : width + half]
    tails = [mm(one_hot(sender, left), tail), mm(one_hot(sender, right), tail)]
    for later in (mesh_ref, cot_ref, w_mesh_ref, node_out_ref, cot_edges_ref):
        later.start()
    w_first_ref.start()
    w_last_ref.start()
    head = head + jnp.concatenate(tails, 1) + local_ref[...].astype(F32)
    v = mm(head.astype(BF), w_mid_ref[...]) + base_ref[...]
    act, slope = silu_parts(v)
    slope_ref[...] = slope
    u = mm(act.astype(BF), w_out_ref[...])
    center = u - jnp.mean(u, -1, keepdims=True)
    rstd = lax.rsqrt(jnp.mean(center * center, -1, keepdims=True) + 1e-05)
    xhat = center * rstd
    xhat_ref[...] = xhat
    rstd_ref[...] = jnp.broadcast_to(rstd, rstd_ref.shape)
    new = (edge_ref[...].astype(F32) + xhat).astype(BF)
    new_ref.put(new)
    to_receiver = one_hot(iota((nodes, edges), 0), receiver_ref[...])
    edge_sum = mm(to_receiver, new).astype(BF)
    terms = mm(grid_sum, w_grid_sum_ref[...]) + mm(edge_sum, w_edge_sum_ref[...])
    sums_ref[...] = terms.astype(BF).reshape(feats, share, width)


def node_kernel(
    sums_ref,
    mesh_ref,
    w_mesh_ref,
    w_edge_sum_ref,
    w_out_ref,
    cot_ref,
    spread_ref,
    new_ref,
    own_ref,
):
    mesh = mesh_ref[...]
    cot = cot_ref[...].astype(F32)
    v = mm(mesh, w_mesh_ref[...]) + jnp.sum(sums_ref[...].astype(F32), axis=0)
    act, slope = silu_parts(v)
    u = mm(act.astype(BF), w_out_ref[...])
    center = u - jnp.mean(u, -1, keepdims=True)
    rstd = lax.rsqrt(jnp.mean(center * center, -1, keepdims=True) + 1e-05)
    xhat = center * rstd
    new_ref[...] = (mesh.astype(F32) + xhat).astype(BF)
    du = norm_back(cot, xhat, rstd)
    dh = mm_nt(du.astype(BF), w_out_ref[...]).astype(BF)
    dv = (dh.astype(F32) * slope).astype(BF)
    sum_grad = mm_nt(dv, w_edge_sum_ref[...]).astype(BF)
    spread_ref[...] = jnp.broadcast_to(sum_grad[None], spread_ref.shape)
    own_ref[...] = cot + mm_nt(dv, w_mesh_ref[...]).astype(BF).astype(F32)


def norm_back(cot, xhat, rstd):
    return rstd * (
        cot
        - jnp.mean(cot, -1, keepdims=True)
        - xhat * jnp.mean(cot * xhat, -1, keepdims=True)
    )


def edge_back_kernel(
    grads_ref,
    cot_ref,
    w_out_ref,
    w_mid_ref,
    sender_ref,
    receiver_ref,
    xhat_ref,
    rstd_ref,
    slope_ref,
    w_first_ref,
    w_last_ref,
    new_ref,
    own_ref,
    send_ref,
    grad_ref,
    local_ref,
    new_again_ref,
    own_again_ref,
    count,
):
    new_again_ref.put(new_ref[...])
    own_again_ref.put(own_ref[...])
    edges, width = cot_ref.shape
    half = width // 2
    nodes = grads_ref.shape[0]
    slots = send_ref.shape[0]
    sender, receiver = sender_ref[...], receiver_ref[...]
    spread = mm(one_hot(column_of(receiver), iota((edges, nodes), 1)), grads_ref[...])
    cot = (cot_ref[...].astype(F32) + spread).astype(BF)
    du = norm_back(cot.astype(F32), xhat_ref[...], rstd_ref[:, 0:1])
    dh = mm_nt(du.astype(BF), w_out_ref[...]).astype(BF)
    dv = (dh.astype(F32) * slope_ref[...]).astype(BF)
    sgrad = mm_nt(dv, w_mid_ref[...]).astype(BF)
    direct = mm_nt(dv, w_first_ref[...]).astype(BF)
    grad_ref.put((cot.astype(F32) + direct.astype(F32)).astype(BF))
    whole, left, right = table_ids((slots, 1), 0, nodes, count)
    send_ref.put(mm(one_hot(whole, sender), sgrad).astype(BF), 0, width)
    tail = mm(one_hot(jnp.maximum(left, right), sender), sgrad)
    tail = jnp.where(left >= 0, tail[:, :half], tail[:, half:]).astype(BF)
    send_ref.put(tail, width, width + half)
    rgrad = mm_nt(dv, w_last_ref[...]).astype(BF)
    ids = iota((nodes, edges), 0)
    local_ref.put(mm(one_hot(ids, sender), sgrad) + mm(one_hot(ids, receiver), rgrad))


def return_kernel(got_ref, halo_ref, local_ref, own_ref, new_ref, out_ref, new_out_ref):
    new_out_ref.put(new_ref[...])
    nodes, width = local_ref.shape
    slots = got_ref.shape[0]
    halo_t = halo_ref[...].reshape(halo_ref.shape[0], slots // 8)
    ids = iota((nodes, slots), 0)
    total = mm(one_hot(ids, halo_row(halo_t, 8, 0)), got_ref[:, :width])
    rest = halo_row(halo_t, 4, 8)
    is_left = iota((1, slots), 1) % 8 < 4
    tail = got_ref[:, width:]
    left = mm(one_hot(ids, jnp.where(is_left, rest, -1)), tail)
    right = mm(one_hot(ids, jnp.where(is_left, -1, rest)), tail)
    total = total + jnp.concatenate([left, right], 1) + local_ref[...]
    out_ref[...] = total.astype(BF).reshape(out_ref.shape)


def finish_kernel(got_ref, own_ref, out_ref):
    out_ref.put((jnp.sum(got_ref[...].astype(F32), axis=0) + own_ref[...]).astype(BF))


def swap(values, axis):
    return lax.all_to_all(values, axis, split_axis=0, concat_axis=0, tiled=True)


def body(
    grid_latents,
    grid_region,
    grid_node,
    mesh_latents,
    edge_latents,
    edge_sender,
    edge_receiver,
    halo_send,
    w_grid,
    w_edge_in,
    w_edge_out,
    w_node_in,
    w_node_out,
    cot_mesh,
    cot_edges,
):
    spaces = lax.axis_size("space")
    feats = lax.axis_size("feat")
    nodes, width = mesh_latents.shape
    edges = edge_latents.shape[0]
    count = halo_send.shape[2]
    share = nodes // feats
    slots = spaces * 8
    back = width + width // 2
    region_row = grid_region.reshape(1, -1)
    node_row = grid_node.reshape(1, -1)
    sender = edge_sender.reshape(1, -1)
    receiver = edge_receiver.reshape(1, -1)
    halo_t = halo_send.transpose(2, 0, 1)
    wide = 2 * width + width // 2 + 128

    def own_start():
        return pl.multiple_of(lax.axis_index("feat") * share, share)

    (packed,) = call(
        pack_kernel,
        [Push((slots, wide), BF)],
        [
            Fetch(array)
            for array in (region_row, node_row, halo_t, mesh_latents, w_grid, grid_latents)
        ],
    )
    got = swap(packed.reshape(spaces, 8, wide), "space").reshape(slots, wide)
    base, sender_local = call(
        ready_kernel,
        [Push((edges, width), F32), Push((edges, width), BF)],
        [Fetch(array) for array in (sender, receiver, mesh_latents, edge_latents, w_edge_in)],
    )
    (
        sums,
        new_edges,
        slope,
        xhat,
        rstd,
        sender_held,
        receiver_held,
        w_mid,
        w_out,
        w_edge_sum,
        mesh_own,
        cot_own,
        w_mesh,
        node_out,
        edge_cot,
        w_first,
        w_last,
    ) = call(
        functools.partial(edge_forward_kernel, count=count),
        [
            ((feats, share, width), BF),
            Push((edges, width), BF),
            ((edges, width), F32),
            ((edges, width), F32),
            ((edges, 128), F32),
        ],
        [
            got,
            Fetch(sender, keep=True),
            Fetch(receiver, keep=True),
            Fetch(sender_local),
            Fetch(w_edge_in, rows=width, start=width, keep=True),
            Fetch(base),
            Fetch(w_edge_out, keep=True),
            Fetch(edge_latents),
            Fetch(w_node_in, rows=width, start=width),
            Fetch(w_node_in, rows=width, start=2 * width, keep=True),
            Fetch(mesh_latents, rows=share, start=own_start, keep=True, defer=True),
            Fetch(cot_mesh, rows=share, start=own_start, keep=True, defer=True),
            Fetch(w_node_in, rows=width, start=0, keep=True, defer=True),
            Fetch(w_node_out, keep=True, defer=True),
            Fetch(cot_edges, keep=True, defer=True),
            Fetch(w_edge_in, rows=width, start=0, keep=True, defer=True),
            Fetch(w_edge_in, rows=width, start=2 * width, keep=True, defer=True),
        ],
    )
    sums = swap(sums, "feat")
    spread, new_share, own = call(
        node_kernel,
        [((feats, share, width), BF), ((share, width), BF), ((share, width), F32)],
        [sums, mesh_own, w_mesh, w_edge_sum, node_out, cot_own],
    )
    grads = swap(spread, "feat").reshape(nodes, width)
    send, grad_edges, local, new_share, own = call(
        functools.partial(edge_back_kernel, count=count),
        [
            Push((slots, back), BF),
            Push((edges, width), BF),
            Push((nodes, width), F32),
            Push((share, width), BF),
            Push((share, width), F32),
        ],
        [
            grads,
            edge_cot,
            w_out,
            w_mid,
            sender_held,
            receiver_held,
            xhat,
            rstd,
            slope,
            w_first,
            w_last,
            new_share,
            own,
        ],
    )
    returned = swap(send.reshape(spaces, 8, back), "space").reshape(slots, back)
    new_mesh = lax.all_gather(new_share, "feat", axis=0, tiled=True)
    parts, new_mesh, own = call(
        return_kernel,
        [((feats, share, width), BF), Push((nodes, width), BF)],
        [
            returned,
            Fetch(halo_t),
            Fetch(local),
            Fetch(own, keep=True),
            new_mesh,
        ],
    )
    last = swap(parts, "feat")
    (grad_mesh,) = call(finish_kernel, [Push((share, width), BF)], [last, own])
    return new_mesh, new_edges, grad_mesh, grad_edges


def solution(mesh):
    return jax.shard_map(
        body,
        mesh=mesh,
        in_specs=(
            P(("space", "feat"), None),
            P(("space", "feat"), None),
            P(("space", "feat")),
            P("space", None),
            P(("space", "feat"), None),
            P(("space", "feat")),
            P(("space", "feat")),
            P("space", None, None),
            P(),
            P(),
            P(),
            P(),
            P(),
            P("space", None),
            P(("space", "feat"), None),
        ),
        out_specs=(
            P("space", None),
            P(("space", "feat"), None),
            P(("space", "feat"), None),
            P(("space", "feat"), None),
        ),
        check_vma=False,
    )
```
